128 devices in a mesh: lat: 4 (over x), lon: 32 (over y, z, core).
Axes of the slice: x: 4, y: 4, z: 4, core: 2. Of those that a mesh axis runs over, the one named last changes fastest.
Arguments:
- tokens: bfloat16 [65536, 1024], P(('lat', 'lon')), may hold values from -60 to 60
- dest_tile: int32 [65536], P(('lat', 'lon')), may hold values from 0 to 128, as said below
- slot_cell: int32 [128, 128, 4], P(('lat', 'lon')), may hold values from 0 to 512, as said below
- w_up: bfloat16 [1024, 4096], replicated, may hold values from -0.1875 to 0.1875
- w_down: bfloat16 [4096, 1024], replicated, may hold values from -0.09375 to 0.09375
- w_proj: bfloat16 [1024, 256], replicated, may hold values from -0.1875 to 0.1875
- w_conv: bfloat16 [3, 3, 256, 256], replicated, may hold values from -0.125 to 0.125
- cotangent: bfloat16 [512, 512, 256], P('lat', 'lon'), may hold values from -6 to 6
Outputs:
- decoded: bfloat16 [512, 512, 256], P('lat', 'lon')
- weight_grad: float32 [3, 3, 256, 256], P(None, None, None, 'lon')
- token_grad: bfloat16 [65536, 256], P(('lat', 'lon'))
The draws below stay inside these ranges and needn't reach their ends.
Inputs may be any that keep to these rules, and one draw needn't show every extreme that they name: `dest_tile`: within a shard the live slots come first and their tiles never decrease. The ocean cells of a tile, in raster order after those of all earlier tiles, are dealt to the shards in turn, so a shard holds a tile's ocean count divided by 128, rounded down or up, and at most 4 tokens for one tile; in every draw some tile is all ocean and receives 4 tokens from every shard. `slot_cell`: entry [d, s, k] names the cell of tile d that receives the token of shard s with dest_tile d and rank k among them, or 512 where shard s has no such token; each cell is named at most once, and the named cells are the tile's ocean cells.
All inputs are finite; a program needn't handle non-finite values.
Results may differ from the reference program's by a relative error of at most 0.0077.
Values may be sent and summed in bfloat16 or wider, within the bound.
A program may use at most 128 MiB of HBM per device.

```python
import math
from functools import partial
import jax
import jax.numpy as jnp
from jax import lax

D = 1024
MLP = 4096
C = 256
TH = 64
TW = 8
TILES = 128
CELLS = 512
TOK_DEV = 512
CAP = 4
TOKENS = 65536
FINE_ROWS = 512
FINE_COLS = 512
N_LAT = 4
N_LON = 32


def layout_tables(key):
    base_key = jax.random.fold_in(key, 7)
    share_key, full_key, roll_key = jax.random.split(base_key, 3)
    ocean_share = jax.random.randint(share_key, (TILES,), 30, 101)
    full_tile = jax.random.randint(full_key, (), 0, TILES)
    ocean_share = jnp.where(jnp.arange(TILES, dtype=jnp.int32) == full_tile, 101, ocean_share)
    rolls = jax.random.randint(roll_key, (TILES, CELLS), 0, 100)
    ocean_mask = (rolls < ocean_share[:, None]).astype(jnp.int32)
    ocean_count = jnp.sum(ocean_mask, axis=1)
    offsets = jnp.cumsum(ocean_count) - ocean_count
    local_rank = jnp.cumsum(ocean_mask, axis=1) - 1
    global_rank = offsets[:, None] + local_rank
    source = jnp.where(ocean_mask == 1, global_rank % TILES, TILES)
    shard_slot = global_rank // TILES
    tile_rank = local_rank // TILES
    tile_ids = jnp.broadcast_to(jnp.arange(TILES, dtype=jnp.int32)[:, None], (TILES, CELLS))
    cell_ids = jnp.broadcast_to(jnp.arange(CELLS, dtype=jnp.int32)[None, :], (TILES, CELLS))
    dest_table = jnp.full((TILES, TOK_DEV), TILES, jnp.int32).at[source, shard_slot].set(tile_ids, mode='drop')
    cell_table = jnp.full((TILES, TILES, CAP), CELLS, jnp.int32).at[tile_ids, source, tile_rank].set(cell_ids, mode='drop')
    return (dest_table.reshape(TOKENS), cell_table)


def draw_dest_tile(key, part):
    return layout_tables(key)[0]


def draw_slot_cell(key, part):
    return layout_tables(key)[1]


def draw_tokens(key, part):
    row_key, col_key, base_key = jax.random.split(jax.random.fold_in(key, 11), 3)
    row_scale = jnp.exp(jax.random.uniform(row_key, (TOKENS, 1), jnp.float32, math.log(0.3), math.log(3.0)))
    col_scale = jnp.exp(jax.random.uniform(col_key, (1, D), jnp.float32, math.log(0.3), math.log(3.0)))
    values = jax.random.normal(base_key, (TOKENS, D), jnp.float32)
    values = jnp.clip(values, -6.0, 6.0)
    return (values * row_scale * col_scale).astype(jnp.bfloat16)


def with_spikes(result, rng, source, target, shards_of, factor):
    def block_of(position):
        return (jnp.arange(result.shape[position]) // (result.shape[position] // shards_of)).reshape((-1,) + (1,) * (result.ndim - 1 - position))

    first = jax.random.permutation(rng, shards_of)[block_of(target)]
    other_side = (block_of(target) + shards_of // 2) % shards_of
    return jnp.where((block_of(source) == first) | (block_of(source) == other_side), factor * result, result)


def level_of(key, extent, cuts, low, high):
    def one(dim, blocks):
        steps = jax.random.uniform(jax.random.fold_in(jax.random.fold_in(key, 6), dim), (blocks,), jnp.float32, low / len(cuts), high / len(cuts))
        return jnp.repeat(jnp.exp(steps), extent[dim] // blocks).reshape((-1,) + (1,) * (len(extent) - dim - 1))

    factor_of = one(*cuts[0])
    for cut in cuts[1:]:
        factor_of = factor_of * one(*cut)
    return factor_of


def noise(rng, extent, width, bound, cuts=(), kind=jnp.bfloat16):
    factor_of = level_of(rng, extent, cuts, -0.22, 0.18) if cuts else 1.0
    values = jax.random.normal(rng, extent, jnp.float32) * width * factor_of
    return jnp.minimum(jnp.maximum(values, -bound), bound).astype(kind)


def heavy_noise(rng, shape, width, bound, pieces, heavy, kind=jnp.bfloat16):
    array = width * jax.random.normal(rng, shape, jnp.float32)
    if pieces:
        array = array * level_of(rng, shape, pieces, -0.22, 0.18)
    return jnp.clip(with_spikes(array, jax.random.fold_in(rng, 3), *heavy), -bound, bound).astype(kind)


def setup_inputs(seed: int = 0) -> dict:
    seeds = jax.random.split(jax.random.key(seed), 9)
    tokens = draw_tokens(jax.random.fold_in(seeds[8], 71), 0)
    dest_tile = draw_dest_tile(jax.random.fold_in(seeds[8], 71), 0)
    slot_cell = draw_slot_cell(jax.random.fold_in(seeds[8], 71), 0)
    w_up = noise(seeds[3], (D, MLP), D ** -0.5, 0.1875)
    w_down = noise(seeds[4], (MLP, D), MLP ** -0.5, 0.09375)
    w_proj = noise(seeds[5], (D, C), D ** -0.5, 0.1875)
    w_conv = noise(seeds[6], (3, 3, C, C), (9 * C) ** -0.5, 0.125)
    cotangent = heavy_noise(seeds[7], (FINE_ROWS, FINE_COLS, C), 1.0, 6.0, ((0, 4), (1, 32)), (1, 2, 32, 2.75))
    return dict(tokens=tokens, dest_tile=dest_tile, slot_cell=slot_cell, w_up=w_up, w_down=w_down, w_proj=w_proj, w_conv=w_conv, cotangent=cotangent)


def encode(rows_in, w_up, w_down):
    values = rows_in.astype(jnp.float32)
    center = values - lax.optimization_barrier(jnp.mean(values, axis=1, keepdims=True))
    spread = lax.optimization_barrier(jnp.mean(center * center, axis=1, keepdims=True))
    normed = (center * lax.rsqrt(spread + 1e-05)).astype(jnp.bfloat16)
    inner_sum = jnp.dot(normed, w_up, preferred_element_type=jnp.float32)
    hidden = jax.nn.gelu(inner_sum, approximate=True).astype(jnp.bfloat16)
    return (values + jnp.dot(hidden, w_down, preferred_element_type=jnp.float32)).astype(jnp.bfloat16)

def periodic_pad(field_in):
    wrapped = jnp.concatenate([field_in[:, -1:], field_in, field_in[:, :1]], axis=1)
    zero_rim = jnp.zeros((1,) + wrapped.shape[1:], field_in.dtype)
    return jnp.concatenate([zero_rim, wrapped, zero_rim], axis=0)

def to_grid(tiled_in):
    depth = tiled_in.shape[-1]
    return tiled_in.reshape(N_LAT, N_LON, TH, TW, depth).transpose(0, 2, 1, 3, 4).reshape(N_LAT * TH, N_LON * TW, depth)

def to_tiles(grid_in):
    depth = grid_in.shape[-1]
    return grid_in.reshape(N_LAT, TH, N_LON, TW, depth).transpose(0, 2, 1, 3, 4).reshape(N_LAT * N_LON, TH * TW, depth)

def reference(tokens, dest_tile, slot_cell, w_up, w_down, w_proj, w_conv, cotangent):
    tile_count = N_LAT * N_LON
    shards = tokens.reshape(tile_count, TOK_DEV, D)

    def project_shard(rows_in):
        return jnp.dot(encode(rows_in, w_up, w_down), w_proj, preferred_element_type=jnp.float32).astype(jnp.bfloat16)
    features = lax.map(project_shard, shards)
    dest_rows = dest_tile.reshape(tile_count, TOK_DEV)
    positions = jnp.arange(TOK_DEV, dtype=jnp.int32)

    def rank_of(row_ids):
        same_dest = jnp.logical_and(row_ids[:, None] == row_ids[None, :], positions[None, :] < positions[:, None])
        return lax.optimization_barrier(jnp.sum(same_dest.astype(jnp.int32), axis=1)).astype(jnp.int32)
    token_rank = lax.map(rank_of, dest_rows)
    source_ids = jnp.broadcast_to(jnp.arange(tile_count, dtype=jnp.int32)[:, None], (tile_count, TOK_DEV))
    token_ids = jnp.broadcast_to(positions[None, :], (tile_count, TOK_DEV))
    slot_token = jnp.full((tile_count, tile_count + 1, CAP), TOK_DEV, jnp.int32)
    slot_token = slot_token.at[source_ids, dest_rows, token_rank].set(token_ids, mode='drop')[:, :tile_count]
    padded_features = jnp.concatenate([features, jnp.zeros((tile_count, 1, C), features.dtype)], axis=1)
    lead_ids = jnp.broadcast_to(jnp.arange(tile_count, dtype=jnp.int32)[:, None, None], (tile_count, tile_count, CAP))
    fetched = padded_features[lead_ids, slot_token]
    latent = jnp.zeros((tile_count, CELLS + 1, C), features.dtype)
    latent = latent.at[lead_ids, slot_cell].set(jnp.transpose(fetched, (1, 0, 2, 3)))[:, :CELLS]
    ocean_cells = jnp.zeros((tile_count, CELLS + 1, 1), jnp.float32).at[lead_ids, slot_cell].set(1.0)[:, :CELLS]
    latent_grid = to_grid(latent)
    wet_grid = to_grid(ocean_cells)
    fine_grid = jnp.repeat(jnp.repeat(latent_grid, 2, axis=0), 2, axis=1)
    wet_fine = jnp.repeat(jnp.repeat(wet_grid, 2, axis=0), 2, axis=1).reshape(-1, 1)
    fine_rows, fine_cols = (fine_grid.shape[0], fine_grid.shape[1])
    framed = periodic_pad(fine_grid)
    mixed_sum = jnp.zeros((fine_rows * fine_cols, C), jnp.float32)
    for row_tap in range(3):
        for col_tap in range(3):
            window = framed[row_tap:row_tap + fine_rows, col_tap:col_tap + fine_cols].reshape(-1, C)
            mixed_sum = mixed_sum + jnp.dot(window, w_conv[row_tap, col_tap], preferred_element_type=jnp.float32)
    activate = partial(jax.nn.gelu, approximate=True)
    activated, pullback = jax.vjp(activate, mixed_sum)
    decoded = (wet_fine * activated).astype(jnp.bfloat16).reshape(fine_rows, fine_cols, C)
    adjoint = pullback(wet_fine * cotangent.reshape(-1, C).astype(jnp.float32))[0].astype(jnp.bfloat16)
    grad_scale = 1.0 / math.sqrt(fine_rows * fine_cols)
    tap_grads = []
    for row_tap in range(3):
        for col_tap in range(3):
            window = framed[row_tap:row_tap + fine_rows, col_tap:col_tap + fine_cols].reshape(-1, C)
            tap_grads.append(lax.dot_general(window, adjoint, (((0,), (0,)), ((), ())), preferred_element_type=jnp.float32))
    weight_grad = jnp.stack(tap_grads).reshape(3, 3, C, C) * grad_scale
    framed_adj = periodic_pad(adjoint.reshape(fine_rows, fine_cols, C))
    fine_grad = jnp.zeros((fine_rows * fine_cols, C), jnp.float32)
    for row_tap in range(3):
        for col_tap in range(3):
            window = framed_adj[2 - row_tap:2 - row_tap + fine_rows, 2 - col_tap:2 - col_tap + fine_cols].reshape(-1, C)
            fine_grad = fine_grad + lax.dot_general(window, w_conv[row_tap, col_tap], (((1,), (1,)), ((), ())), preferred_element_type=jnp.float32)
    cell_grad = fine_grad.reshape(fine_rows // 2, 2, fine_cols // 2, 2, C).sum(axis=(1, 3)).astype(jnp.bfloat16)
    tiled_grad = to_tiles(cell_grad)
    padded_grad = jnp.concatenate([tiled_grad, jnp.zeros((tile_count, 1, C), tiled_grad.dtype)], axis=1)
    returned = padded_grad[lead_ids, slot_cell]
    token_grad = jnp.zeros((tile_count, TOK_DEV + 1, C), jnp.bfloat16)
    token_grad = token_grad.at[lead_ids, slot_token].set(jnp.transpose(returned, (1, 0, 2, 3)))[:, :TOK_DEV]
    return (decoded, weight_grad, token_grad.reshape(TOKENS, C))
```

```python
import functools
import math

import jax
import jax.numpy as jnp
from jax import lax
from jax.experimental import pallas as pl
from jax.experimental.pallas import tpu as pltpu
from jax.sharding import PartitionSpec as P

F32 = jnp.float32
BF16 = jnp.bfloat16
MESH = pl.DeviceIdType.MESH

D = 1024
MLP = 4096
C = 256
CAP = 4
TOK = 512
LAT = 4
LON = 32
STEPS = 8
BLOCK = MLP // STEPS
ROW_CHOICES = (336, 352, 384, 512)

W = 10
ROWS = 656
PADDED = 768
GELU_C = math.sqrt(2.0 / math.pi)
GELU_K = 0.044715


def gelu(x):
    return 0.5 * x * (1.0 + jnp.tanh(x * (GELU_C + (GELU_C * GELU_K) * (x * x))))


def iota(shape, dim):
    return lax.broadcasted_iota(jnp.int32, shape, dim)


def one_hot(left, right):
    return jnp.where(left == right, 1.0, 0.0).astype(BF16)


def encode_kernel(
    dest_smem, dest_ref, tokens, w_up, w_down, w_proj, out_ref, target_ref,
    tok_v, up_v, down_v, normed, acc, tok_sem, up_sem, down_sem,
):
    tok_copy = pltpu.make_async_copy(tokens, tok_v, tok_sem)
    tok_copy.start()

    def copies(j):
        return (
            pltpu.make_async_copy(
                w_up.at[:, pl.ds(pl.multiple_of(j * BLOCK, BLOCK), BLOCK)], up_v.at[j], up_sem.at[j]
            ),
            pltpu.make_async_copy(
                w_down.at[pl.ds(pl.multiple_of(j * BLOCK, BLOCK), BLOCK), :], down_v.at[j], down_sem.at[j]
            ),
        )

    for j in range(STEPS):
        for copy in copies(j):
            copy.start()

    dest = jnp.broadcast_to(dest_ref[...], (8, TOK))
    place = iota((8, TOK), 1)
    rank = jnp.zeros((8, TOK), jnp.int32)
    for back in range(1, CAP):
        same = jnp.logical_and(pltpu.roll(dest, back, 1) == dest, place >= back)
        rank = rank + jnp.where(same, 1, 0)
    target = jnp.where(dest < LAT * LON, dest * CAP + rank, -2)
    target_ref[...] = target
    tok_copy.wait()

    def run(rows):
        values = tok_v[:rows, :].astype(F32)
        center = values - jnp.mean(values, axis=1, keepdims=True)
        spread = jnp.mean(center * center, axis=1, keepdims=True)
        normed[:rows, :] = (center * lax.rsqrt(spread + 1e-05)).astype(BF16)
        acc[:rows, :] = values

        def step(j, carry):
            up, down = copies(j)
            up.wait()
            inner = jnp.dot(normed[:rows, :], up_v[j], preferred_element_type=F32)
            hidden = gelu(inner).astype(BF16)
            down.wait()
            acc[:rows, :] += jnp.dot(hidden, down_v[j], preferred_element_type=F32)
            return carry

        lax.fori_loop(0, STEPS, step, 0)
        payload = jnp.dot(
            acc[:rows, :].astype(BF16), w_proj[...], preferred_element_type=F32
        ).astype(BF16)
        selector = one_hot(iota((LAT * LON * CAP, rows), 0), target[:1, :rows])
        out_ref[...] = jnp.dot(selector, payload, preferred_element_type=F32).astype(BF16)

    below = False
    for place, rows in enumerate(ROW_CHOICES):
        fits = True if rows == TOK else dest_smem[rows] >= LAT * LON
        if place == 0:
            pl.when(fits)(functools.partial(run, rows))
            below = fits
        elif rows == TOK:
            pl.when(jnp.logical_not(below))(functools.partial(run, rows))
        else:
            pl.when(jnp.logical_and(fits, jnp.logical_not(below)))(functools.partial(run, rows))
            below = jnp.logical_or(below, fits)


def grid_kernel(
    outgoing, target_ref, slot_ref, w_conv, cot,
    decoded, wgrad, tgrad,
    r1, s2, r2, wc, pad, x, ct, a_all, a_own, z, cg, gt, dw, sa, ra, sb, rb, sd, rd,
    perm, place_m, gather_m, se, hc, hr, cse, chc, chr_,
    s3, r3, s4, r4,
    s1_ss, s1_rs, s2_ss, s2_rs, ch_ss, ch_rs, lh_ss, lh_rs, s3_ss, s3_rs, s4_ss, s4_rs,
    a_ss, a_rs, b_ss, b_rs, d_ss, d_rs,
):
    a = lax.axis_index("lat")
    b = lax.axis_index("lon")
    core = lax.rem(b, 2)
    chip = b // 2
    a_up, a_dn = lax.rem(a + LAT - 1, LAT), lax.rem(a + 1, LAT)
    b_lf, b_rt = lax.rem(b + LON - 1, LON), lax.rem(b + 1, LON)
    mate = b + 1 - 2 * core

    def remote(src, dst, ss, rs, dev):
        return pltpu.make_async_remote_copy(
            src_ref=src, dst_ref=dst, send_sem=ss, recv_sem=rs, device_id=dev, device_id_type=MESH
        )

    barrier = pltpu.get_barrier_semaphore()

    def greet(dev):
        pl.semaphore_signal(barrier, inc=1, device_id=dev, device_id_type=MESH)

    for k in range(1, LAT):
        greet((lax.rem(a + k, LAT), b))

    def greet_lon(k, carry):
        greet((a, lax.rem(b + k, LON)))
        return carry

    lax.fori_loop(1, LON, greet_lon, 0)
    for aa in (a_up, a_dn):
        for bb in (b_lf, b_rt):
            greet((aa, bb))
    for k in range(1, LAT):
        greet((lax.rem(a + k, LAT), mate))
    pl.semaphore_wait(barrier, (LAT - 1) + (LON - 1) + 4 + (LAT - 1))

    def copy1(k):
        to = lax.rem(a + k, LAT)
        return remote(outgoing.at[to], r1.at[a], s1_ss.at[to], s1_rs.at[a], (to, b))

    def recv1(k):
        fr = lax.rem(a + LAT - k, LAT)
        return remote(outgoing.at[fr], r1.at[fr], s1_ss.at[fr], s1_rs.at[fr], (fr, b))

    for k in range(1, LAT):
        copy1(k).start()
    r1[a] = outgoing[a]

    ct[...] = jnp.zeros_like(ct)

    def fill(t, carry):
        even = cot[2 * t].astype(F32)
        odd = cot[2 * t + 1].astype(F32)
        for h in range(2):
            lanes = slice(h * 128, h * 128 + 128)
            ct[0, h, pl.ds(t * (2 * W) + 1, 16), :] = even[:, lanes]
            ct[1, h, pl.ds(t * (2 * W) + (2 * W) + 1, 16), :] = odd[:, lanes]
        return carry

    lax.fori_loop(0, 64, fill, 0, unroll=4)
    for side, col in enumerate((1, 16)):
        for i in range(2):
            for h in range(2):
                cse[side, pl.ds(64 * i, 64), h * 128 : h * 128 + 128] = ct[
                    i, h, pl.ds(i * 2 * W + col, 64, stride=2 * W), :
                ].astype(BF16)

    row_moves = (
        ("bottom", a_dn, b, 0), ("bottom", a_dn, b_rt, 1), ("bottom", a_dn, b_lf, 2),
        ("top", a_up, b, 3), ("top", a_up, b_rt, 4), ("top", a_up, b_lf, 5),
    )

    def halo_copies(cols, rows, col_dst, row_dst, ss, rs):
        moves = [
            remote(cols(1), col_dst.at[0], ss.at[0], rs.at[0], (a, b_rt)),
            remote(cols(0), col_dst.at[1], ss.at[1], rs.at[1], (a, b_lf)),
        ]
        for name, aa, bb, slot in row_moves:
            moves.append(
                remote(rows(name), row_dst.at[slot], ss.at[2 + slot], rs.at[2 + slot], (aa, bb))
            )
        return moves

    cot_moves = halo_copies(
        lambda side: cse.at[side],
        lambda name: cot.at[0] if name == "top" else cot.at[127],
        chc, chr_, ch_ss, ch_rs,
    )
    for move in cot_moves:
        move.start()

    row, col = iota((TOK, TOK), 0), iota((TOK, TOK), 1)
    perm[0] = one_hot(((row >> 2) & 3) * 128 + (row >> 4) * 4 + (row & 3), col)
    perm[1] = one_hot(((col >> 2) & 3) * 128 + (col >> 4) * 4 + (col & 3), row)

    for k in range(1, LAT):
        recv1(k).wait_recv()
    mixed_rows = jnp.dot(perm[0], r1[...].reshape(TOK, C), preferred_element_type=F32)
    s2[...] = mixed_rows.astype(BF16).reshape(LON, 16, C)

    def lon_copy(src, dst, ss, rs, k):
        to = lax.rem(b + k, LON)
        return remote(src.at[to], dst.at[b], ss.at[to], rs.at[b], (a, to))

    def lon_recv(src, dst, ss, rs, k):
        fr = lax.rem(b + LON - k, LON)
        return remote(src.at[fr], dst.at[fr], ss.at[fr], rs.at[fr], (a, fr))

    def loop(lo, hi, body):
        def step(k, carry):
            body(k)
            return carry

        lax.fori_loop(lo, hi, step, 0)

    loop(1, LON, lambda k: lon_copy(s2, r2, s2_ss, s2_rs, k).start())
    r2[b] = s2[b]

    combos = {(0, 0): (0,), (1, 0): (1, 2), (0, 1): (0, 1), (1, 1): (2,)}
    for dr in range(2):
        for dq in range(2):
            for i in range(2):
                for j in range(2):
                    total = None
                    for ka in combos[dr, i]:
                        for kb in combos[dq, j]:
                            term = w_conv[3 * ka + kb].astype(F32)
                            total = term if total is None else total + term
                    wc[
                        (2 * dr + dq) * C : (2 * dr + dq + 1) * C, (2 * i + j) * C : (2 * i + j + 1) * C
                    ] = total.astype(BF16)

    slot = jnp.broadcast_to(slot_ref[...], (128, TOK))
    flat_row = jnp.where(slot < TOK, ((slot >> 3) + 1) * W + (slot & 7) + 1, -2)[:1, :]
    place_m[160:832, :] = one_hot(iota((672, TOK), 0), flat_row)
    edge = iota((160, 1), 0)
    cell = jnp.where(
        edge < 64, edge * 8,
        jnp.where(
            edge < 128, (edge - 64) * 8 + 7,
            jnp.where(
                edge < 144, jnp.where(edge < 136, edge - 128, -2),
                jnp.where(edge < 152, edge - 144 + 504, -2),
            ),
        ),
    )
    place_m[0:160, :] = one_hot(cell, slot[:1, :])
    flat_col = jnp.where(slot < TOK, ((slot >> 3) + 1) * W + (slot & 7) + 1, -2).astype(F32).T
    for blk in range(PADDED // 128):
        gather_m[:, blk * 128 : blk * 128 + 128] = one_hot(
            flat_col, (iota((TOK, 128), 1) + blk * 128).astype(F32)
        )
    x[ROWS:, :] = jnp.zeros((PADDED - ROWS, 4 * C), BF16)
    a_own[ROWS:, :] = jnp.zeros((PADDED - ROWS, 4 * C), BF16)
    cg[ROWS:, :] = jnp.zeros((PADDED - ROWS, C), BF16)
    z[0:16, :] = jnp.zeros((16, 4 * C), F32)
    pad[:, 672:, :] = jnp.zeros((3, 8, 128), F32)

    keep_top = jnp.where(a > 0, 1.0, 0.0)
    keep_bot = jnp.where(a < LAT - 1, 1.0, 0.0)

    for move in cot_moves:
        move.wait()
    for h in range(2):
        lanes = slice(h * 128, h * 128 + 128)
        for i in range(2):
            for side, at in ((0, 0), (1, 17)):
                ct[i, h, pl.ds(i * 2 * W + at, 64, stride=2 * W), :] = chc[
                    side, pl.ds(64 * i, 64), lanes
                ].astype(F32)
        for base, i, t, keep in ((0, 1, 0, keep_top), (3, 0, 64, keep_bot)):
            ct[i, h, t * 2 * W + 1 : t * 2 * W + 17, :] = chr_[base, :, lanes].astype(F32) * keep
            ct[i, h, t * 2 * W : t * 2 * W + 1, :] = (
                chr_[base + 1, :, lanes].astype(F32)[15:16, :] * keep
            )
            ct[i, h, t * 2 * W + 17 : t * 2 * W + 18, :] = (
                chr_[base + 2, :, lanes].astype(F32)[0:1, :] * keep
            )

    loop(1, LON, lambda k: lon_recv(s2, r2, s2_ss, s2_rs, k).wait_recv())
    arrived = jnp.concatenate(
        [r2[...].reshape(TOK, C), jnp.ones((TOK, 128), BF16)], axis=1
    )
    se[...] = jnp.dot(place_m[0:160, :], arrived, preferred_element_type=F32).astype(BF16)
    lat_moves = halo_copies(
        lambda side: se.at[pl.ds(64 * side, 64)],
        lambda name: se.at[pl.ds(128, 16)] if name == "top" else se.at[pl.ds(144, 16)],
        hc, hr, lh_ss, lh_rs,
    )
    for move in lat_moves:
        move.start()
    placed = jnp.dot(place_m[160:832, :], arrived, preferred_element_type=F32)
    for lane in range(3):
        pad[lane, 0:672, :] = placed[:, lane * 128 : lane * 128 + 128]
    for move in lat_moves:
        move.wait()
    for lane in range(3):
        lanes = slice(lane * 128, lane * 128 + 128)
        for side, at in ((0, 0), (1, W - 1)):
            pad[lane, pl.ds(W + at, 64, stride=W), :] = hc[side, :, lanes].astype(F32)
        for base, t, keep in ((0, 0, keep_top), (3, 65, keep_bot)):
            pad[lane, t * W + 1 : t * W + 9, :] = hr[base, :, lanes].astype(F32)[0:8, :] * keep
            pad[lane, t * W : t * W + 1, :] = hr[base + 1, :, lanes].astype(F32)[7:8, :] * keep
            pad[lane, t * W + 9 : t * W + 10, :] = hr[base + 2, :, lanes].astype(F32)[0:1, :] * keep

    for dr in range(2):
        for dq in range(2):
            at = dr * W + dq
            for h in range(2):
                lo = (2 * dr + dq) * C + h * 128
                x[0:ROWS, lo : lo + 128] = pad[h, at : at + ROWS, :].astype(BF16)

    flat = iota((ROWS, 128), 0)
    t_of = (flat * 6554) >> 16
    u_of = flat - t_of * W
    for i in range(2):
        for j in range(2):
            ph = 2 * i + j
            mixed = jnp.dot(x[0:ROWS, :], wc[:, ph * C : ph * C + C], preferred_element_type=F32)
            at = (1 - i) * W + (1 - j)
            wet = pad[2, at : at + ROWS, :]
            inside = jnp.logical_and(
                jnp.logical_and(t_of >= i, t_of < 64 + i), jnp.logical_and(u_of >= j, u_of < 8 + j)
            )
            for h in range(2):
                m = mixed[:, h * 128 : h * 128 + 128]
                square = m * m
                half = 0.5 + 0.5 * jnp.tanh(m * (GELU_C + (GELU_C * GELU_K) * square))
                slope = half + m * (half * (1.0 - half)) * (
                    2.0 * GELU_C + (6.0 * GELU_C * GELU_K) * square
                )
                spot = pl.ds(1 - j, ROWS, stride=2)
                adj = wet * ct[i, h, spot, :] * slope
                ct[i, h, spot, :] = wet * (m * half)
                lo = ph * C + h * 128
                a_all[0:ROWS, lo : lo + 128] = adj.astype(BF16)
                a_own[0:ROWS, lo : lo + 128] = jnp.where(inside, adj, 0.0).astype(BF16)
            gt[ph] = lax.dot_general(
                a_own[:, ph * C : ph * C + C], x[...], (((0,), (0,)), ((), ())),
                preferred_element_type=F32,
            )

    picks = (((0, 0), (1, 0)), ((0, 1), (1, 0)), ((0, 1), (1, 1)))
    scale = 1.0 / 512.0
    for ka in range(3):
        for kb in range(3):
            for h in range(2):
                total = None
                for i, dr in picks[ka]:
                    for j, dq in picks[kb]:
                        lo = (2 * dr + dq) * C + h * 128
                        term = gt[2 * i + j, :, lo : lo + 128]
                        total = term if total is None else total + term
                total = total * scale
                dw[h, 3 * ka + kb] = total
                sa[h, 3 * ka + kb] = total.astype(BF16)
    move_a = remote(sa.at[1 - core], ra, a_ss.at[0], a_rs.at[0], (a, mate))
    move_a.start()

    z[16 : 16 + ROWS, :] = lax.dot_general(
        a_all[0:ROWS, :], wc[...], (((1,), (1,)), ((), ())), preferred_element_type=F32
    )
    total = None
    for dr in range(2):
        for dq in range(2):
            at = 16 - dr * W - dq
            lo = (2 * dr + dq) * C
            term = z[at : at + ROWS, lo : lo + C]
            total = term if total is None else total + term
    cg[0:ROWS, :] = total.astype(BF16)
    sending = jnp.dot(gather_m[...], cg[...], preferred_element_type=F32)
    s3[...] = sending.astype(BF16).reshape(LON, 16, C)
    loop(1, LON, lambda k: lon_copy(s3, r3, s3_ss, s3_rs, k).start())
    r3[b] = s3[b]

    move_a.wait()
    for tap in range(9):
        pair = dw[core, tap] + ra[tap].astype(F32)
        sb[:, tap] = pair.astype(BF16).reshape(16, 16, 128)

    def copy_b(k):
        to = lax.rem(chip + k, 16)
        return remote(sb.at[to], rb.at[chip], b_ss.at[to], b_rs.at[chip], (a, 2 * to + core))

    def recv_b(k):
        fr = lax.rem(chip + 16 - k, 16)
        return remote(sb.at[fr], rb.at[fr], b_ss.at[fr], b_rs.at[fr], (a, 2 * fr + core))

    loop(1, 16, lambda k: copy_b(k).start())
    rb[chip] = sb[chip]

    target_col = jnp.broadcast_to(target_ref[...][:1, :], (128, TOK)).astype(F32).T
    for blk in range(4):
        place_m[0:TOK, blk * 128 : blk * 128 + 128] = one_hot(
            target_col, (iota((TOK, 128), 1) + blk * 128).astype(F32)
        )

    def emit(t, carry):
        for i in range(2):
            at = (t + i) * (2 * W) + 1
            decoded[2 * t + i] = jnp.concatenate(
                [ct[i, 0, pl.ds(at, 16), :], ct[i, 1, pl.ds(at, 16), :]], axis=1
            ).astype(BF16)
        return carry

    lax.fori_loop(0, 64, emit, 0, unroll=4)

    loop(1, LON, lambda k: lon_recv(s3, r3, s3_ss, s3_rs, k).wait_recv())
    back = jnp.dot(perm[1], r3[...].reshape(TOK, C), preferred_element_type=F32)
    s4[...] = back.astype(BF16).reshape(LAT, 128, C)

    def copy4(k):
        to = lax.rem(a + k, LAT)
        return remote(s4.at[to], r4.at[a], s4_ss.at[to], s4_rs.at[a], (to, b))

    def recv4(k):
        fr = lax.rem(a + LAT - k, LAT)
        return remote(s4.at[fr], r4.at[fr], s4_ss.at[fr], s4_rs.at[fr], (fr, b))

    for k in range(1, LAT):
        copy4(k).start()
    r4[a] = s4[a]

    loop(1, 16, lambda k: recv_b(k).wait_recv())
    for tap in range(9):
        plane = rb[0, tap].astype(F32)
        for m in range(1, 16):
            plane = plane + rb[m, tap].astype(F32)
        sd[0, tap] = plane[0:8, :]
        sd[1, tap] = plane[8:16, :]

    def pair_of(k, c):
        return lax.rem(a + k, LAT), lax.rem(core + c, 2)

    def copy_d(k, c):
        aa, cc = pair_of(k, c)
        return remote(
            sd.at[cc], rd.at[core, a], d_ss.at[cc, aa], d_rs.at[core, a], (aa, 2 * chip + cc)
        )

    def recv_d(k, c):
        aa, cc = pair_of(LAT - k, c)
        return remote(
            sd.at[cc], rd.at[cc, aa], d_ss.at[cc, aa], d_rs.at[cc, aa], (aa, 2 * chip + cc)
        )

    others = [(k, c) for c in range(2) for k in range(LAT) if (k, c) != (0, 0)]
    for k, c in others:
        copy_d(k, c).start()
    rd[core, a] = sd[core]

    for k in range(1, LAT):
        recv4(k).wait_recv()
    tgrad[...] = jnp.dot(
        place_m[0:TOK, :], r4[...].reshape(TOK, C), preferred_element_type=F32
    ).astype(BF16)

    for k, c in others:
        recv_d(k, c).wait_recv()
    for c in range(2):
        wgrad[:, :, c * 128 : c * 128 + 128] = (rd[c, 0] + rd[c, 1]) + (rd[c, 2] + rd[c, 3])

    for k in range(1, LAT):
        copy1(k).wait_send()
        copy4(k).wait_send()
    loop(1, LON, lambda k: lon_copy(s2, r2, s2_ss, s2_rs, k).wait_send())
    loop(1, LON, lambda k: lon_copy(s3, r3, s3_ss, s3_rs, k).wait_send())
    loop(1, 16, lambda k: copy_b(k).wait_send())
    for k, c in others:
        copy_d(k, c).wait_send()


def local(tokens, dest_tile, slot_cell, w_up, w_down, w_proj, w_conv, cotangent):
    vmem = pl.BlockSpec(memory_space=pltpu.VMEM)
    smem = pl.BlockSpec(memory_space=pltpu.SMEM)
    hbm = pl.BlockSpec(memory_space=pl.ANY)
    dma = pltpu.SemaphoreType.DMA
    outgoing, target = pl.pallas_call(
        encode_kernel,
        out_shape=(
            jax.ShapeDtypeStruct((TOK, C), BF16),
            jax.ShapeDtypeStruct((8, TOK), jnp.int32),
        ),
        in_specs=[smem, vmem, hbm, hbm, hbm, vmem],
        out_specs=(vmem, vmem),
        scratch_shapes=[
            pltpu.VMEM((TOK, D), BF16),
            pltpu.VMEM((STEPS, D, BLOCK), BF16),
            pltpu.VMEM((STEPS, BLOCK, D), BF16),
            pltpu.VMEM((TOK, D), BF16),
            pltpu.VMEM((TOK, D), F32),
            dma,
            dma((STEPS,)),
            dma((STEPS,)),
        ],
        compiler_params=pltpu.CompilerParams(vmem_limit_bytes=48 * 1024 * 1024),
        cost_estimate=pl.CostEstimate(
            flops=17_000_000_000, bytes_accessed=19_000_000, transcendentals=2_000_000
        ),
        name="encode",
    )(dest_tile, dest_tile.reshape(1, TOK), tokens, w_up, w_down, w_proj)

    slots = slot_cell.reshape(LAT, LON, CAP).transpose(1, 0, 2).reshape(1, TOK)
    v = pltpu.VMEM
    decoded, wgrad, tgrad = pl.pallas_call(
        grid_kernel,
        out_shape=(
            jax.ShapeDtypeStruct((128, 16, C), BF16),
            jax.ShapeDtypeStruct((9, 8, C), F32),
            jax.ShapeDtypeStruct((TOK, C), BF16),
        ),
        in_specs=[vmem] * 5,
        out_specs=(vmem, vmem, vmem),
        scratch_shapes=[
            v((LAT, 128, C), BF16),
            v((LON, 16, C), BF16),
            v((LON, 16, C), BF16),
            v((4 * C, 4 * C), BF16),
            v((3, 680, 128), F32),
            v((PADDED, 4 * C), BF16),
            v((2, 2, 2 * ROWS, 128), F32),
            v((PADDED, 4 * C), BF16),
            v((PADDED, 4 * C), BF16),
            v((16 + ROWS, 4 * C), F32),
            v((PADDED, C), BF16),
            v((4, C, 4 * C), F32),
            v((2, 9, C, 128), F32),
            v((2, 9, C, 128), BF16),
            v((9, C, 128), BF16),
            v((16, 9, 16, 128), BF16),
            v((16, 9, 16, 128), BF16),
            v((2, 9, 8, 128), F32),
            v((2, LAT, 9, 8, 128), F32),
            v((2, TOK, TOK), BF16),
            v((832, TOK), BF16),
            v((TOK, PADDED), BF16),
            v((160, C + 128), BF16),
            v((2, 64, C + 128), BF16),
            v((6, 16, C + 128), BF16),
            v((2, 128, C), BF16),
            v((2, 128, C), BF16),
            v((6, 16, C), BF16),
            v((LON, 16, C), BF16),
            v((LON, 16, C), BF16),
            v((LAT, 128, C), BF16),
            v((LAT, 128, C), BF16),
            dma((LAT,)), dma((LAT,)), dma((LON,)), dma((LON,)), dma((8,)), dma((8,)),
            dma((8,)), dma((8,)), dma((LON,)), dma((LON,)), dma((LAT,)), dma((LAT,)),
            dma((1,)), dma((1,)), dma((16,)), dma((16,)), dma((2, LAT)), dma((2, LAT)),
        ],
        compiler_params=pltpu.CompilerParams(
            collective_id=0, has_side_effects=True, vmem_limit_bytes=56 * 1024 * 1024
        ),
        cost_estimate=pl.CostEstimate(
            flops=5_000_000_000, bytes_accessed=4_000_000, transcendentals=600_000
        ),
        name="grid",
    )(
        outgoing.reshape(LAT, 128, C), target, slots, w_conv.reshape(9, C, C), cotangent
    )
    weight_grad = wgrad.reshape(3, 3, 8, C).transpose(0, 1, 3, 2)
    return decoded, weight_grad, tgrad


def solution(mesh):
    in_specs = (
        P(("lat", "lon"), None),
        P(("lat", "lon")),
        P(("lat", "lon"), None, None),
        P(),
        P(),
        P(),
        P(),
        P("lat", "lon", None),
    )
    out_specs = (P("lat", "lon", None), P(None, None, None, "lon"), P(("lat", "lon"), None))
    return jax.shard_map(local, mesh=mesh, in_specs=in_specs, out_specs=out_specs, check_vma=False)
```

```python
import functools
import math

import jax
import jax.numpy as jnp
from jax import lax
from jax.experimental import pallas as pl
from jax.experimental.pallas import tpu as pltpu
from jax.sharding import PartitionSpec as P

F32 = jnp.float32
BF16 = jnp.bfloat16
MESH = pl.DeviceIdType.MESH

D = 1024
MLP = 4096
C = 256
CAP = 4
TOK = 512
LAT = 4
LON = 32
STEPS = 8
BLOCK = MLP // STEPS
RING = 5

W = 10
ROWS = 656
PADDED = 768
GELU_C = math.sqrt(2.0 / math.pi)
GELU_K = 0.044715


def gelu(x):
    return 0.5 * x * (1.0 + jnp.tanh(x * (GELU_C + (GELU_C * GELU_K) * (x * x))))


def iota(shape, dim):
    return lax.broadcasted_iota(jnp.int32, shape, dim)


def one_hot(left, right):
    return jnp.where(left == right, 1.0, 0.0).astype(BF16)


def grid_kernel(
    tokens_h, dest_h, slot_h, w_up, w_down, w_proj_h, w_conv_h, cot_h,
    decoded, wgrad, tgrad,
    tok_v, up_v, down_v, normed, acc, inner, dest_v, slot_v, w_proj, w_conv, cot, outgoing,
    tok_sem, up_sem, down_sem, in_sem,
    r1, s2, r2, wc, pad, x, ct, a_all, a_own, z, cg, gt, dw, sa, ra, sb, rb, sd, rd,
    perm, place_m, gather_m, se, hc, hr, cse, chc, chr_,
    s3, r3, s4, r4,
    s1_ss, s1_rs, s2_ss, s2_rs, ch_ss, ch_rs, lh_ss, lh_rs, s3_ss, s3_rs, s4_ss, s4_rs,
    a_ss, a_rs, b_ss, b_rs, d_ss, d_rs,
):
    a = lax.axis_index("lat")
    b = lax.axis_index("lon")
    core = lax.rem(b, 2)
    chip = b // 2
    a_up, a_dn = lax.rem(a + LAT - 1, LAT), lax.rem(a + 1, LAT)
    b_lf, b_rt = lax.rem(b + LON - 1, LON), lax.rem(b + 1, LON)
    mate = b + 1 - 2 * core

    def remote(src, dst, ss, rs, dev):
        return pltpu.make_async_remote_copy(
            src_ref=src, dst_ref=dst, send_sem=ss, recv_sem=rs, device_id=dev, device_id_type=MESH
        )

    small = [
        pltpu.make_async_copy(src, dst, in_sem.at[n])
        for n, (src, dst) in enumerate((
            (dest_h, dest_v), (slot_h, slot_v), (w_proj_h, w_proj), (cot_h, cot), (w_conv_h, w_conv)
        ))
    ]
    tok_copies = [
        pltpu.make_async_copy(
            tokens_h.at[pl.ds(n * 128, 128), :], tok_v.at[pl.ds(n * 128, 128), :], tok_sem.at[n]
        )
        for n in range(4)
    ]

    def up_copy(j):
        at = lax.rem(j, RING)
        lo = pl.multiple_of(j * BLOCK, BLOCK)
        return pltpu.make_async_copy(w_up.at[:, pl.ds(lo, BLOCK)], up_v.at[at], up_sem.at[at])

    def down_copy(j):
        at = lax.rem(j, RING)
        lo = pl.multiple_of(j * BLOCK, BLOCK)
        return pltpu.make_async_copy(w_down.at[pl.ds(lo, BLOCK), :], down_v.at[at], down_sem.at[at])

    for copy in tok_copies:
        copy.start()
    up_copy(0).start()
    for n in range(2):
        small[n].start()
    up_copy(1).start()
    down_copy(0).start()
    for n in range(2, RING):
        up_copy(n).start()
        down_copy(n - 1).start()
    down_copy(RING - 1).start()

    barrier = pltpu.get_barrier_semaphore()

    def greet(dev):
        pl.semaphore_signal(barrier, inc=1, device_id=dev, device_id_type=MESH)

    for k in range(1, LAT):
        greet((lax.rem(a + k, LAT), b))

    def greet_lon(k, carry):
        greet((a, lax.rem(b + k, LON)))
        return carry

    lax.fori_loop(1, LON, greet_lon, 0)
    for aa in (a_up, a_dn):
        for bb in (b_lf, b_rt):
            greet((aa, bb))
    for k in range(1, LAT):
        greet((lax.rem(a + k, LAT), mate))

    for copy in small[2:]:
        copy.start()

    small[0].wait()
    small[1].wait()
    dest = jnp.broadcast_to(dest_v[...], (8, TOK))
    place = iota((8, TOK), 1)
    rank = jnp.zeros((8, TOK), jnp.int32)
    for step in range(1, CAP):
        same = jnp.logical_and(pltpu.roll(dest, step, 1) == dest, place >= step)
        rank = rank + jnp.where(same, 1, 0)
    target = jnp.where(dest < LAT * LON, dest * CAP + rank, -2)[:1, :]
    order = iota((128, TOK), 1)
    spread = one_hot(((order >> 2) & 3) * LON + (order >> 4), iota((128, TOK), 0))
    by_rank = slot_v[...]
    spread_of = lambda part: jnp.dot(
        part.astype(F32).astype(BF16), spread, preferred_element_type=F32
    )
    moved = 8.0 * spread_of(by_rank >> 3) + spread_of(by_rank & 7)
    rank_is = (iota((CAP, TOK), 1) & 3) == iota((CAP, TOK), 0)
    slot_row = jnp.sum(jnp.where(rank_is, moved, 0.0), axis=0, keepdims=True).astype(jnp.int32)

    for n in range(4):
        tok_copies[n].wait()
        rows = slice(n * 128, n * 128 + 128)
        values = tok_v[rows, :].astype(F32)
        center = values - jnp.mean(values, axis=1, keepdims=True)
        variance = jnp.mean(center * center, axis=1, keepdims=True)
        normed[rows, :] = (center * lax.rsqrt(variance + 1e-05)).astype(BF16)
        acc[rows, :] = values
    up_copy(0).wait()
    inner[0] = jnp.dot(normed[...], up_v[0], preferred_element_type=F32)

    def hidden_step(j, last):
        if not last:
            up_copy(j + 1).wait()
        down_copy(j).wait()
        if not last:
            inner[lax.rem(j + 1, 2)] = jnp.dot(
                normed[...], up_v[lax.rem(j + 1, RING)], preferred_element_type=F32
            )
        hidden = gelu(inner[lax.rem(j, 2)]).astype(BF16)
        acc[...] += jnp.dot(hidden, down_v[lax.rem(j, RING)], preferred_element_type=F32)

    def refill_step(j, carry):
        hidden_step(j, False)

        @pl.when(j + RING < STEPS)
        def _():
            up_copy(j + RING).start()
            down_copy(j + RING).start()

        return carry

    lax.fori_loop(0, STEPS - 1, refill_step, 0)
    hidden_step(STEPS - 1, True)
    small[2].wait()
    payload = jnp.dot(acc[...].astype(BF16), w_proj[...], preferred_element_type=F32).astype(BF16)
    selector = one_hot(iota((TOK, TOK), 0), target)
    outgoing[...] = (
        jnp.dot(selector, payload, preferred_element_type=F32).astype(BF16).reshape(LAT, 128, C)
    )
    pl.semaphore_wait(barrier, (LAT - 1) + (LON - 1) + 4 + (LAT - 1))

    def copy1(k):
        to = lax.rem(a + k, LAT)
        return remote(outgoing.at[to], r1.at[a], s1_ss.at[to], s1_rs.at[a], (to, b))

    def recv1(k):
        fr = lax.rem(a + LAT - k, LAT)
        return remote(outgoing.at[fr], r1.at[fr], s1_ss.at[fr], s1_rs.at[fr], (fr, b))

    for k in range(1, LAT):
        copy1(k).start()
    r1[a] = outgoing[a]

    small[3].wait()
    ct[...] = jnp.zeros_like(ct)

    def fill(t, carry):
        even = cot[2 * t].astype(F32)
        odd = cot[2 * t + 1].astype(F32)
        for h in range(2):
            lanes = slice(h * 128, h * 128 + 128)
            ct[0, h, pl.ds(t * (2 * W) + 1, 16), :] = even[:, lanes]
            ct[1, h, pl.ds(t * (2 * W) + (2 * W) + 1, 16), :] = odd[:, lanes]
        return carry

    lax.fori_loop(0, 64, fill, 0, unroll=4)
    for side, col in enumerate((1, 16)):
        for i in range(2):
            for h in range(2):
                cse[side, pl.ds(64 * i, 64), h * 128 : h * 128 + 128] = ct[
                    i, h, pl.ds(i * 2 * W + col, 64, stride=2 * W), :
                ].astype(BF16)

    row_moves = (
        ("bottom", a_dn, b, 0), ("bottom", a_dn, b_rt, 1), ("bottom", a_dn, b_lf, 2),
        ("top", a_up, b, 3), ("top", a_up, b_rt, 4), ("top", a_up, b_lf, 5),
    )

    def halo_copies(cols, rows, col_dst, row_dst, ss, rs):
        moves = [
            remote(cols(1), col_dst.at[0], ss.at[0], rs.at[0], (a, b_rt)),
            remote(cols(0), col_dst.at[1], ss.at[1], rs.at[1], (a, b_lf)),
        ]
        for name, aa, bb, slot in row_moves:
            moves.append(
                remote(rows(name), row_dst.at[slot], ss.at[2 + slot], rs.at[2 + slot], (aa, bb))
            )
        return moves

    cot_moves = halo_copies(
        lambda side: cse.at[side],
        lambda name: cot.at[0] if name == "top" else cot.at[127],
        chc, chr_, ch_ss, ch_rs,
    )
    for move in cot_moves:
        move.start()

    row, col = iota((TOK, TOK), 0), iota((TOK, TOK), 1)
    perm[0] = one_hot(((row >> 2) & 3) * 128 + (row >> 4) * 4 + (row & 3), col)
    perm[1] = one_hot(((col >> 2) & 3) * 128 + (col >> 4) * 4 + (col & 3), row)

    for k in range(1, LAT):
        recv1(k).wait_recv()
    mixed_rows = jnp.dot(perm[0], r1[...].reshape(TOK, C), preferred_element_type=F32)
    s2[...] = mixed_rows.astype(BF16).reshape(LON, 16, C)

    def lon_copy(src, dst, ss, rs, k):
        to = lax.rem(b + k, LON)
        return remote(src.at[to], dst.at[b], ss.at[to], rs.at[b], (a, to))

    def lon_recv(src, dst, ss, rs, k):
        fr = lax.rem(b + LON - k, LON)
        return remote(src.at[fr], dst.at[fr], ss.at[fr], rs.at[fr], (a, fr))

    def loop(lo, hi, body):
        def step(k, carry):
            body(k)
            return carry

        lax.fori_loop(lo, hi, step, 0)

    loop(1, LON, lambda k: lon_copy(s2, r2, s2_ss, s2_rs, k).start())
    r2[b] = s2[b]

    small[4].wait()
    combos = {(0, 0): (0,), (1, 0): (1, 2), (0, 1): (0, 1), (1, 1): (2,)}
    for dr in range(2):
        for dq in range(2):
            for i in range(2):
                for j in range(2):
                    total = None
                    for ka in combos[dr, i]:
                        for kb in combos[dq, j]:
                            term = w_conv[3 * ka + kb].astype(F32)
                            total = term if total is None else total + term
                    wc[
                        (2 * dr + dq) * C : (2 * dr + dq + 1) * C, (2 * i + j) * C : (2 * i + j + 1) * C
                    ] = total.astype(BF16)

    slot = jnp.broadcast_to(slot_row, (128, TOK))
    flat_row = jnp.where(slot < TOK, ((slot >> 3) + 1) * W + (slot & 7) + 1, -2)[:1, :]
    place_m[160:832, :] = one_hot(iota((672, TOK), 0), flat_row)
    edge = iota((160, 1), 0)
    cell = jnp.where(
        edge < 64, edge * 8,
        jnp.where(
            edge < 128, (edge - 64) * 8 + 7,
            jnp.where(
                edge < 144, jnp.where(edge < 136, edge - 128, -2),
                jnp.where(edge < 152, edge - 144 + 504, -2),
            ),
        ),
    )
    place_m[0:160, :] = one_hot(cell, slot[:1, :])
    flat_col = jnp.where(slot < TOK, ((slot >> 3) + 1) * W + (slot & 7) + 1, -2).astype(F32).T
    for blk in range(PADDED // 128):
        gather_m[:, blk * 128 : blk * 128 + 128] = one_hot(
            flat_col, (iota((TOK, 128), 1) + blk * 128).astype(F32)
        )
    x[ROWS:, :] = jnp.zeros((PADDED - ROWS, 4 * C), BF16)
    a_own[ROWS:, :] = jnp.zeros((PADDED - ROWS, 4 * C), BF16)
    cg[ROWS:, :] = jnp.zeros((PADDED - ROWS, C), BF16)
    z[0:16, :] = jnp.zeros((16, 4 * C), F32)
    pad[:, 672:, :] = jnp.zeros((3, 8, 128), F32)

    keep_top = jnp.where(a > 0, 1.0, 0.0)
    keep_bot = jnp.where(a < LAT - 1, 1.0, 0.0)

    for move in cot_moves:
        move.wait()
    for h in range(2):
        lanes = slice(h * 128, h * 128 + 128)
        for i in range(2):
            for side, at in ((0, 0), (1, 17)):
                ct[i, h, pl.ds(i * 2 * W + at, 64, stride=2 * W), :] = chc[
                    side, pl.ds(64 * i, 64), lanes
                ].astype(F32)
        for base, i, t, keep in ((0, 1, 0, keep_top), (3, 0, 64, keep_bot)):
            ct[i, h, t * 2 * W + 1 : t * 2 * W + 17, :] = chr_[base, :, lanes].astype(F32) * keep
            ct[i, h, t * 2 * W : t * 2 * W + 1, :] = (
                chr_[base + 1, :, lanes].astype(F32)[15:16, :] * keep
            )
            ct[i, h, t * 2 * W + 17 : t * 2 * W + 18, :] = (
                chr_[base + 2, :, lanes].astype(F32)[0:1, :] * keep
            )

    loop(1, LON, lambda k: lon_recv(s2, r2, s2_ss, s2_rs, k).wait_recv())
    arrived = jnp.concatenate(
        [r2[...].reshape(TOK, C), jnp.ones((TOK, 128), BF16)], axis=1
    )
    se[...] = jnp.dot(place_m[0:160, :], arrived, preferred_element_type=F32).astype(BF16)
    lat_moves = halo_copies(
        lambda side: se.at[pl.ds(64 * side, 64)],
        lambda name: se.at[pl.ds(128, 16)] if name == "top" else se.at[pl.ds(144, 16)],
        hc, hr, lh_ss, lh_rs,
    )
    for move in lat_moves:
        move.start()
    placed = jnp.dot(place_m[160:832, :], arrived, preferred_element_type=F32)
    for lane in range(3):
        pad[lane, 0:672, :] = placed[:, lane * 128 : lane * 128 + 128]
    for move in lat_moves:
        move.wait()
    for lane in range(3):
        lanes = slice(lane * 128, lane * 128 + 128)
        for side, at in ((0, 0), (1, W - 1)):
            pad[lane, pl.ds(W + at, 64, stride=W), :] = hc[side, :, lanes].astype(F32)
        for base, t, keep in ((0, 0, keep_top), (3, 65, keep_bot)):
            pad[lane, t * W + 1 : t * W + 9, :] = hr[base, :, lanes].astype(F32)[0:8, :] * keep
            pad[lane, t * W : t * W + 1, :] = hr[base + 1, :, lanes].astype(F32)[7:8, :] * keep
            pad[lane, t * W + 9 : t * W + 10, :] = hr[base + 2, :, lanes].astype(F32)[0:1, :] * keep

    for dr in range(2):
        for dq in range(2):
            at = dr * W + dq
            for h in range(2):
                lo = (2 * dr + dq) * C + h * 128
                x[0:ROWS, lo : lo + 128] = pad[h, at : at + ROWS, :].astype(BF16)

    flat = iota((ROWS, 128), 0)
    t_of = (flat * 6554) >> 16
    u_of = flat - t_of * W
    for i in range(2):
        for j in range(2):
            ph = 2 * i + j
            mixed = jnp.dot(x[0:ROWS, :], wc[:, ph * C : ph * C + C], preferred_element_type=F32)
            at = (1 - i) * W + (1 - j)
            wet = pad[2, at : at + ROWS, :]
            inside = jnp.logical_and(
                jnp.logical_and(t_of >= i, t_of < 64 + i), jnp.logical_and(u_of >= j, u_of < 8 + j)
            )
            for h in range(2):
                m = mixed[:, h * 128 : h * 128 + 128]
                square = m * m
                half = 0.5 + 0.5 * jnp.tanh(m * (GELU_C + (GELU_C * GELU_K) * square))
                slope = half + m * (half * (1.0 - half)) * (
                    2.0 * GELU_C + (6.0 * GELU_C * GELU_K) * square
                )
                spot = pl.ds(1 - j, ROWS, stride=2)
                adj = wet * ct[i, h, spot, :] * slope
                ct[i, h, spot, :] = wet * (m * half)
                lo = ph * C + h * 128
                a_all[0:ROWS, lo : lo + 128] = adj.astype(BF16)
                a_own[0:ROWS, lo : lo + 128] = jnp.where(inside, adj, 0.0).astype(BF16)
            gt[ph] = lax.dot_general(
                a_own[:, ph * C : ph * C + C], x[...], (((0,), (0,)), ((), ())),
                preferred_element_type=F32,
            )

    picks = (((0, 0), (1, 0)), ((0, 1), (1, 0)), ((0, 1), (1, 1)))
    scale = 1.0 / 512.0
    for ka in range(3):
        for kb in range(3):
            for h in range(2):
                total = None
                for i, dr in picks[ka]:
                    for j, dq in picks[kb]:
                        lo = (2 * dr + dq) * C + h * 128
                        term = gt[2 * i + j, :, lo : lo + 128]
                        total = term if total is None else total + term
                total = total * scale
                dw[h, 3 * ka + kb] = total
                sa[h, 3 * ka + kb] = total.astype(BF16)
    move_a = remote(sa.at[1 - core], ra, a_ss.at[0], a_rs.at[0], (a, mate))
    move_a.start()

    z[16 : 16 + ROWS, :] = lax.dot_general(
        a_all[0:ROWS, :], wc[...], (((1,), (1,)), ((), ())), preferred_element_type=F32
    )
    total = None
    for dr in range(2):
        for dq in range(2):
            at = 16 - dr * W - dq
            lo = (2 * dr + dq) * C
            term = z[at : at + ROWS, lo : lo + C]
            total = term if total is None else total + term
    cg[0:ROWS, :] = total.astype(BF16)
    sending = jnp.dot(gather_m[...], cg[...], preferred_element_type=F32)
    s3[...] = sending.astype(BF16).reshape(LON, 16, C)
    loop(1, LON, lambda k: lon_copy(s3, r3, s3_ss, s3_rs, k).start())
    r3[b] = s3[b]

    move_a.wait()
    for tap in range(9):
        pair = dw[core, tap] + ra[tap].astype(F32)
        sb[:, tap] = pair.astype(BF16).reshape(16, 16, 128)

    def copy_b(k):
        to = lax.rem(chip + k, 16)
        return remote(sb.at[to], rb.at[chip], b_ss.at[to], b_rs.at[chip], (a, 2 * to + core))

    def recv_b(k):
        fr = lax.rem(chip + 16 - k, 16)
        return remote(sb.at[fr], rb.at[fr], b_ss.at[fr], b_rs.at[fr], (a, 2 * fr + core))

    loop(1, 16, lambda k: copy_b(k).start())
    rb[chip] = sb[chip]

    target_col = jnp.broadcast_to(target, (128, TOK)).astype(F32).T
    for blk in range(4):
        place_m[0:TOK, blk * 128 : blk * 128 + 128] = one_hot(
            target_col, (iota((TOK, 128), 1) + blk * 128).astype(F32)
        )

    def emit(t, carry):
        for i in range(2):
            at = (t + i) * (2 * W) + 1
            decoded[2 * t + i] = jnp.concatenate(
                [ct[i, 0, pl.ds(at, 16), :], ct[i, 1, pl.ds(at, 16), :]], axis=1
            ).astype(BF16)
        return carry

    lax.fori_loop(0, 64, emit, 0, unroll=4)

    loop(1, LON, lambda k: lon_recv(s3, r3, s3_ss, s3_rs, k).wait_recv())
    back = jnp.dot(perm[1], r3[...].reshape(TOK, C), preferred_element_type=F32)
    s4[...] = back.astype(BF16).reshape(LAT, 128, C)

    def copy4(k):
        to = lax.rem(a + k, LAT)
        return remote(s4.at[to], r4.at[a], s4_ss.at[to], s4_rs.at[a], (to, b))

    def recv4(k):
        fr = lax.rem(a + LAT - k, LAT)
        return remote(s4.at[fr], r4.at[fr], s4_ss.at[fr], s4_rs.at[fr], (fr, b))

    for k in range(1, LAT):
        copy4(k).start()
    r4[a] = s4[a]

    loop(1, 16, lambda k: recv_b(k).wait_recv())
    for tap in range(9):
        plane = rb[0, tap].astype(F32)
        for m in range(1, 16):
            plane = plane + rb[m, tap].astype(F32)
        sd[0, tap] = plane[0:8, :]
        sd[1, tap] = plane[8:16, :]

    def pair_of(k, c):
        return lax.rem(a + k, LAT), lax.rem(core + c, 2)

    def copy_d(k, c):
        aa, cc = pair_of(k, c)
        return remote(
            sd.at[cc], rd.at[core, a], d_ss.at[cc, aa], d_rs.at[core, a], (aa, 2 * chip + cc)
        )

    def recv_d(k, c):
        aa, cc = pair_of(LAT - k, c)
        return remote(
            sd.at[cc], rd.at[cc, aa], d_ss.at[cc, aa], d_rs.at[cc, aa], (aa, 2 * chip + cc)
        )

    others = [(k, c) for c in range(2) for k in range(LAT) if (k, c) != (0, 0)]
    for k, c in others:
        copy_d(k, c).start()
    rd[core, a] = sd[core]

    for k in range(1, LAT):
        recv4(k).wait_recv()
    tgrad[...] = jnp.dot(
        place_m[0:TOK, :], r4[...].reshape(TOK, C), preferred_element_type=F32
    ).astype(BF16)

    for k, c in others:
        recv_d(k, c).wait_recv()
    for c in range(2):
        wgrad[:, :, c * 128 : c * 128 + 128] = (rd[c, 0] + rd[c, 1]) + (rd[c, 2] + rd[c, 3])

    for k in range(1, LAT):
        copy1(k).wait_send()
        copy4(k).wait_send()
    loop(1, LON, lambda k: lon_copy(s2, r2, s2_ss, s2_rs, k).wait_send())
    loop(1, LON, lambda k: lon_copy(s3, r3, s3_ss, s3_rs, k).wait_send())
    loop(1, 16, lambda k: copy_b(k).wait_send())
    for k, c in others:
        copy_d(k, c).wait_send()


def hand_over_kernel(decoded, wgrad, tgrad, decoded_out, wgrad_out, tgrad_out, sems):
    copies = [
        pltpu.make_async_copy(
            decoded.at[pl.ds(n * 32, 32)], decoded_out.at[pl.ds(n * 32, 32)], sems.at[n]
        )
        for n in range(4)
    ]
    copies.append(pltpu.make_async_copy(wgrad, wgrad_out, sems.at[4]))
    copies.append(pltpu.make_async_copy(tgrad, tgrad_out, sems.at[5]))
    for copy in copies:
        copy.start()
    for copy in copies:
        copy.wait()


def local(tokens, dest_tile, slot_cell, w_up, w_down, w_proj, w_conv, cotangent):
    vmem = pl.BlockSpec(memory_space=pltpu.VMEM)
    hbm = pl.BlockSpec(memory_space=pltpu.HBM)
    dma = pltpu.SemaphoreType.DMA
    v = pltpu.VMEM
    decoded, wgrad, tgrad = pl.pallas_call(
        grid_kernel,
        out_shape=(v((128, 16, C), BF16), v((9, 8, C), F32), v((TOK, C), BF16)),
        in_specs=[hbm] * 8,
        out_specs=(vmem, vmem, vmem),
        scratch_shapes=[
            v((TOK, D), BF16),
            v((RING, D, BLOCK), BF16),
            v((RING, BLOCK, D), BF16),
            v((TOK, D), BF16),
            v((TOK, D), F32),
            v((2, TOK, BLOCK), F32),
            v((1, TOK), jnp.int32),
            v((CAP, 128), jnp.int32),
            v((D, C), BF16),
            v((9, C, C), BF16),
            v((128, 16, C), BF16),
            v((LAT, 128, C), BF16),
            dma((4,)), dma((RING,)), dma((RING,)), dma((5,)),
            v((LAT, 128, C), BF16),
            v((LON, 16, C), BF16),
            v((LON, 16, C), BF16),
            v((4 * C, 4 * C), BF16),
            v((3, 680, 128), F32),
            v((PADDED, 4 * C), BF16),
            v((2, 2, 2 * ROWS, 128), F32),
            v((PADDED, 4 * C), BF16),
            v((PADDED, 4 * C), BF16),
            v((16 + ROWS, 4 * C), F32),
            v((PADDED, C), BF16),
            v((4, C, 4 * C), F32),
            v((2, 9, C, 128), F32),
            v((2, 9, C, 128), BF16),
            v((9, C, 128), BF16),
            v((16, 9, 16, 128), BF16),
            v((16, 9, 16, 128), BF16),
            v((2, 9, 8, 128), F32),
            v((2, LAT, 9, 8, 128), F32),
            v((2, TOK, TOK), BF16),
            v((832, TOK), BF16),
            v((TOK, PADDED), BF16),
            v((160, C + 128), BF16),
            v((2, 64, C + 128), BF16),
            v((6, 16, C + 128), BF16),
            v((2, 128, C), BF16),
            v((2, 128, C), BF16),
            v((6, 16, C), BF16),
            v((LON, 16, C), BF16),
            v((LON, 16, C), BF16),
            v((LAT, 128, C), BF16),
            v((LAT, 128, C), BF16),
            dma((LAT,)), dma((LAT,)), dma((LON,)), dma((LON,)), dma((8,)), dma((8,)),
            dma((8,)), dma((8,)), dma((LON,)), dma((LON,)), dma((LAT,)), dma((LAT,)),
            dma((1,)), dma((1,)), dma((16,)), dma((16,)), dma((2, LAT)), dma((2, LAT)),
        ],
        compiler_params=pltpu.CompilerParams(
            collective_id=0, has_side_effects=True, vmem_limit_bytes=58 * 1024 * 1024
        ),
        cost_estimate=pl.CostEstimate(
            flops=22_000_000_000, bytes_accessed=24_000_000, transcendentals=2_600_000
        ),
        name="grid",
    )(
        tokens, dest_tile.reshape(1, TOK), slot_cell.reshape(LAT * LON, CAP).T, w_up, w_down, w_proj,
        w_conv.reshape(9, C, C), cotangent,
    )
    decoded, wgrad, tgrad = pl.pallas_call(
        hand_over_kernel,
        out_shape=(
            jax.ShapeDtypeStruct((128, 16, C), BF16),
            jax.ShapeDtypeStruct((9, 8, C), F32),
            jax.ShapeDtypeStruct((TOK, C), BF16),
        ),
        in_specs=[vmem] * 3,
        out_specs=(hbm, hbm, hbm),
        scratch_shapes=[dma((6,))],
        name="hand_over",
    )(decoded, wgrad, tgrad)
    weight_grad = wgrad.reshape(3, 3, 8, C).transpose(0, 1, 3, 2)
    return decoded, weight_grad, tgrad


def solution(mesh):
    in_specs = (
        P(("lat", "lon"), None),
        P(("lat", "lon")),
        P(("lat", "lon"), None, None),
        P(),
        P(),
        P(),
        P(),
        P("lat", "lon", None),
    )
    out_specs = (P("lat", "lon", None), P(None, None, None, "lon"), P(("lat", "lon"), None))
    return jax.shard_map(local, mesh=mesh, in_specs=in_specs, out_specs=out_specs, check_vma=False)
```

```python
import functools
import math

import jax
import jax.numpy as jnp
from jax import lax
from jax.experimental import pallas as pl
from jax.experimental.pallas import tpu as pltpu
from jax.sharding import PartitionSpec as P

F32 = jnp.float32
BF16 = jnp.bfloat16
MESH = pl.DeviceIdType.MESH

D = 1024
MLP = 4096
C = 256
CAP = 4
TOK = 512
LAT = 4
LON = 32
STEPS = 4
BLOCK = MLP // STEPS
RING = 3

W = 10
ROWS = 656
PADDED = 768
GELU_C = math.sqrt(2.0 / math.pi)
GELU_K = 0.044715


def gelu(x):
    return 0.5 * x * (1.0 + jnp.tanh(x * (GELU_C + (GELU_C * GELU_K) * (x * x))))


def iota(shape, dim):
    return lax.broadcasted_iota(jnp.int32, shape, dim)


def one_hot(left, right):
    return jnp.where(left == right, 1.0, 0.0).astype(BF16)


def grid_kernel(
    tokens_h, dest_h, slot_h, w_up, w_down, w_proj_h, w_conv_h, cot_h,
    decoded, wgrad, tgrad,
    tok_v, up_v, down_v, normed, acc, inner_0, inner_1, dest_v, slot_v, w_proj, w_conv, cot, outgoing,
    tok_sem, up_sem, down_sem, in_sem,
    r1, s2, r2, wc, pad, x, ct, a_all, a_own, z, cg, gt, dw, sa, ra, sb, rb, sx, rx, sy, ry, sd, rd,
    perm, place_m, gather_m, se, hc, hr, cse, chc, chr_,
    s3, r3, s4, r4,
    s1_ss, s1_rs, s2_ss, s2_rs, ch_ss, ch_rs, lh_ss, lh_rs, s3_ss, s3_rs, s4_ss, s4_rs,
    a_ss, a_rs, b_ss, b_rs, d_ss, d_rs, x_ss, x_rs, y_ss, y_rs,
):
    a = lax.axis_index("lat")
    b = lax.axis_index("lon")
    core = lax.rem(b, 2)
    chip = b // 2
    a_up, a_dn = lax.rem(a + LAT - 1, LAT), lax.rem(a + 1, LAT)
    b_lf, b_rt = lax.rem(b + LON - 1, LON), lax.rem(b + 1, LON)
    mate = b + 1 - 2 * core

    def remote(src, dst, ss, rs, dev):
        return pltpu.make_async_remote_copy(
            src_ref=src, dst_ref=dst, send_sem=ss, recv_sem=rs, device_id=dev, device_id_type=MESH
        )

    small = [
        pltpu.make_async_copy(src, dst, in_sem.at[n])
        for n, (src, dst) in enumerate((
            (dest_h, dest_v), (slot_h, slot_v), (w_proj_h, w_proj), (cot_h, cot), (w_conv_h, w_conv)
        ))
    ]
    tok_copies = [
        pltpu.make_async_copy(
            tokens_h.at[pl.ds(n * 128, 128), :], tok_v.at[pl.ds(n * 128, 128), :], tok_sem.at[n]
        )
        for n in range(4)
    ]

    def up_copy(j):
        at = j % RING
        return pltpu.make_async_copy(w_up.at[:, pl.ds(j * BLOCK, BLOCK)], up_v.at[at], up_sem.at[at])

    def down_copy(j):
        at = j % RING
        return pltpu.make_async_copy(w_down.at[pl.ds(j * BLOCK, BLOCK), :], down_v.at[at], down_sem.at[at])

    for copy in tok_copies:
        copy.start()
    up_copy(0).start()
    for n in range(2):
        small[n].start()
    up_copy(1).start()
    down_copy(0).start()
    for n in range(2, RING):
        up_copy(n).start()
        down_copy(n - 1).start()
    down_copy(RING - 1).start()

    barrier = pltpu.get_barrier_semaphore()

    def greet(dev):
        pl.semaphore_signal(barrier, inc=1, device_id=dev, device_id_type=MESH)

    for k in range(1, LAT):
        greet((lax.rem(a + k, LAT), b))

    def greet_lon(k, carry):
        greet((a, lax.rem(b + k, LON)))
        return carry

    lax.fori_loop(1, LON, greet_lon, 0)
    for aa in (a_up, a_dn):
        for bb in (b_lf, b_rt):
            greet((aa, bb))
    for k in range(1, LAT):
        greet((lax.rem(a + k, LAT), mate))

    for copy in small[2:]:
        copy.start()

    small[0].wait()
    small[1].wait()
    dest = jnp.broadcast_to(dest_v[...], (8, TOK))
    place = iota((8, TOK), 1)
    rank = jnp.zeros((8, TOK), jnp.int32)
    for step in range(1, CAP):
        same = jnp.logical_and(pltpu.roll(dest, step, 1) == dest, place >= step)
        rank = rank + jnp.where(same, 1, 0)
    target = jnp.where(dest < LAT * LON, dest * CAP + rank, -2)[:1, :]
    order = iota((128, TOK), 1)
    spread = one_hot(((order >> 2) & 3) * LON + (order >> 4), iota((128, TOK), 0))
    by_rank = slot_v[...]
    spread_of = lambda part: jnp.dot(
        part.astype(F32).astype(BF16), spread, preferred_element_type=F32
    )
    moved = 8.0 * spread_of(by_rank >> 3) + spread_of(by_rank & 7)
    rank_is = (iota((CAP, TOK), 1) & 3) == iota((CAP, TOK), 0)
    slot_row = jnp.sum(jnp.where(rank_is, moved, 0.0), axis=0, keepdims=True).astype(jnp.int32)

    inner = (inner_0, inner_1)
    for n in range(4):
        tok_copies[n].wait()
        rows = slice(n * 128, n * 128 + 128)
        values = tok_v[rows, :].astype(F32)
        center = values - jnp.mean(values, axis=1, keepdims=True)
        variance = jnp.mean(center * center, axis=1, keepdims=True)
        normed[rows, :] = (center * lax.rsqrt(variance + 1e-05)).astype(BF16)
        acc[rows, :] = values
    up_copy(0).wait()
    inner[0][...] = jnp.dot(normed[...], up_v[0], preferred_element_type=F32)

    for j in range(STEPS):
        last = j == STEPS - 1
        if not last:
            up_copy(j + 1).wait()
        down_copy(j).wait()
        hidden = gelu(inner[j % 2][...]).astype(BF16)
        if not last:
            inner[(j + 1) % 2][...] = jnp.dot(
                normed[...], up_v[(j + 1) % RING], preferred_element_type=F32
            )
        acc[...] += jnp.dot(hidden, down_v[j % RING], preferred_element_type=F32)
        if j + RING < STEPS:
            up_copy(j + RING).start()
            down_copy(j + RING).start()
    small[2].wait()
    payload = jnp.dot(acc[...].astype(BF16), w_proj[...], preferred_element_type=F32).astype(BF16)
    selector = one_hot(iota((TOK, TOK), 0), target)
    outgoing[...] = (
        jnp.dot(selector, payload, preferred_element_type=F32).astype(BF16).reshape(LAT, 128, C)
    )
    pl.semaphore_wait(barrier, (LAT - 1) + (LON - 1) + 4 + (LAT - 1))

    def copy1(k):
        to = lax.rem(a + k, LAT)
        return remote(outgoing.at[to], r1.at[a], s1_ss.at[to], s1_rs.at[a], (to, b))

    def recv1(k):
        fr = lax.rem(a + LAT - k, LAT)
        return remote(outgoing.at[fr], r1.at[fr], s1_ss.at[fr], s1_rs.at[fr], (fr, b))

    for k in range(1, LAT):
        copy1(k).start()
    r1[a] = outgoing[a]

    small[3].wait()
    ct[...] = jnp.zeros_like(ct)

    def fill(t, carry):
        even = cot[2 * t].astype(F32)
        odd = cot[2 * t + 1].astype(F32)
        for h in range(2):
            lanes = slice(h * 128, h * 128 + 128)
            ct[0, h, pl.ds(t * (2 * W) + 1, 16), :] = even[:, lanes]
            ct[1, h, pl.ds(t * (2 * W) + (2 * W) + 1, 16), :] = odd[:, lanes]
        return carry

    lax.fori_loop(0, 64, fill, 0, unroll=4)
    for side, col in enumerate((1, 16)):
        for i in range(2):
            for h in range(2):
                cse[side, pl.ds(64 * i, 64), h * 128 : h * 128 + 128] = ct[
                    i, h, pl.ds(i * 2 * W + col, 64, stride=2 * W), :
                ].astype(BF16)

    row_moves = (
        ("bottom", a_dn, b, 0), ("bottom", a_dn, b_rt, 1), ("bottom", a_dn, b_lf, 2),
        ("top", a_up, b, 3), ("top", a_up, b_rt, 4), ("top", a_up, b_lf, 5),
    )

    def halo_copies(cols, rows, col_dst, row_dst, ss, rs):
        moves = [
            remote(cols(1), col_dst.at[0], ss.at[0], rs.at[0], (a, b_rt)),
            remote(cols(0), col_dst.at[1], ss.at[1], rs.at[1], (a, b_lf)),
        ]
        for name, aa, bb, slot in row_moves:
            moves.append(
                remote(rows(name), row_dst.at[slot], ss.at[2 + slot], rs.at[2 + slot], (aa, bb))
            )
        return moves

    cot_moves = halo_copies(
        lambda side: cse.at[side],
        lambda name: cot.at[0] if name == "top" else cot.at[127],
        chc, chr_, ch_ss, ch_rs,
    )
    for move in cot_moves:
        move.start()

    row, col = iota((TOK, TOK), 0), iota((TOK, TOK), 1)
    perm[0] = one_hot(((row >> 2) & 3) * 128 + (row >> 4) * 4 + (row & 3), col)
    perm[1] = one_hot(((col >> 2) & 3) * 128 + (col >> 4) * 4 + (col & 3), row)

    for k in range(1, LAT):
        recv1(k).wait_recv()
    mixed_rows = jnp.dot(perm[0], r1[...].reshape(TOK, C), preferred_element_type=F32)
    s2[...] = mixed_rows.astype(BF16).reshape(LON, 16, C)

    def lon_copy(src, dst, ss, rs, k):
        to = lax.rem(b + k, LON)
        return remote(src.at[to], dst.at[b], ss.at[to], rs.at[b], (a, to))

    def lon_recv(src, dst, ss, rs, k):
        fr = lax.rem(b + LON - k, LON)
        return remote(src.at[fr], dst.at[fr], ss.at[fr], rs.at[fr], (a, fr))

    def loop(lo, hi, body):
        def step(k, carry):
            body(k)
            return carry

        lax.fori_loop(lo, hi, step, 0)

    loop(1, LON, lambda k: lon_copy(s2, r2, s2_ss, s2_rs, k).start())
    r2[b] = s2[b]

    small[4].wait()
    combos = {(0, 0): (0,), (1, 0): (1, 2), (0, 1): (0, 1), (1, 1): (2,)}
    for dr in range(2):
        for dq in range(2):
            for i in range(2):
                for j in range(2):
                    total = None
                    for ka in combos[dr, i]:
                        for kb in combos[dq, j]:
                            term = w_conv[3 * ka + kb].astype(F32)
                            total = term if total is None else total + term
                    wc[
                        (2 * dr + dq) * C : (2 * dr + dq + 1) * C, (2 * i + j) * C : (2 * i + j + 1) * C
                    ] = total.astype(BF16)

    slot = jnp.broadcast_to(slot_row, (128, TOK))
    flat_row = jnp.where(slot < TOK, ((slot >> 3) + 1) * W + (slot & 7) + 1, -2)[:1, :]
    place_m[160:832, :] = one_hot(iota((672, TOK), 0), flat_row)
    edge = iota((160, 1), 0)
    cell = jnp.where(
        edge < 64, edge * 8,
        jnp.where(
            edge < 128, (edge - 64) * 8 + 7,
            jnp.where(
                edge < 144, jnp.where(edge < 136, edge - 128, -2),
                jnp.where(edge < 152, edge - 144 + 504, -2),
            ),
        ),
    )
    place_m[0:160, :] = one_hot(cell, slot[:1, :])
    flat_col = jnp.where(slot < TOK, ((slot >> 3) + 1) * W + (slot & 7) + 1, -2).astype(F32).T
    for blk in range(PADDED // 128):
        gather_m[:, blk * 128 : blk * 128 + 128] = one_hot(
            flat_col, (iota((TOK, 128), 1) + blk * 128).astype(F32)
        )
    x[ROWS:, :] = jnp.zeros((PADDED - ROWS, 4 * C), BF16)
    a_own[ROWS:, :] = jnp.zeros((PADDED - ROWS, 4 * C), BF16)
    cg[ROWS:, :] = jnp.zeros((PADDED - ROWS, C), BF16)
    z[0:16, :] = jnp.zeros((16, 4 * C), F32)
    pad[:, 672:, :] = jnp.zeros((3, 8, 128), F32)

    keep_top = jnp.where(a > 0, 1.0, 0.0)
    keep_bot = jnp.where(a < LAT - 1, 1.0, 0.0)

    for move in cot_moves:
        move.wait()
    for h in range(2):
        lanes = slice(h * 128, h * 128 + 128)
        for i in range(2):
            for side, at in ((0, 0), (1, 17)):
                ct[i, h, pl.ds(i * 2 * W + at, 64, stride=2 * W), :] = chc[
                    side, pl.ds(64 * i, 64), lanes
                ].astype(F32)
        for base, i, t, keep in ((0, 1, 0, keep_top), (3, 0, 64, keep_bot)):
            ct[i, h, t * 2 * W + 1 : t * 2 * W + 17, :] = chr_[base, :, lanes].astype(F32) * keep
            ct[i, h, t * 2 * W : t * 2 * W + 1, :] = (
                chr_[base + 1, :, lanes].astype(F32)[15:16, :] * keep
            )
            ct[i, h, t * 2 * W + 17 : t * 2 * W + 18, :] = (
                chr_[base + 2, :, lanes].astype(F32)[0:1, :] * keep
            )

    loop(1, LON, lambda k: lon_recv(s2, r2, s2_ss, s2_rs, k).wait_recv())
    arrived = jnp.concatenate(
        [r2[...].reshape(TOK, C), jnp.ones((TOK, 128), BF16)], axis=1
    )
    se[...] = jnp.dot(place_m[0:160, :], arrived, preferred_element_type=F32).astype(BF16)
    lat_moves = halo_copies(
        lambda side: se.at[pl.ds(64 * side, 64)],
        lambda name: se.at[pl.ds(128, 16)] if name == "top" else se.at[pl.ds(144, 16)],
        hc, hr, lh_ss, lh_rs,
    )
    for move in lat_moves:
        move.start()
    placed = jnp.dot(place_m[160:832, :], arrived, preferred_element_type=F32)
    for lane in range(3):
        pad[lane, 0:672, :] = placed[:, lane * 128 : lane * 128 + 128]
    for move in lat_moves:
        move.wait()
    for lane in range(3):
        lanes = slice(lane * 128, lane * 128 + 128)
        for side, at in ((0, 0), (1, W - 1)):
            pad[lane, pl.ds(W + at, 64, stride=W), :] = hc[side, :, lanes].astype(F32)
        for base, t, keep in ((0, 0, keep_top), (3, 65, keep_bot)):
            pad[lane, t * W + 1 : t * W + 9, :] = hr[base, :, lanes].astype(F32)[0:8, :] * keep
            pad[lane, t * W : t * W + 1, :] = hr[base + 1, :, lanes].astype(F32)[7:8, :] * keep
            pad[lane, t * W + 9 : t * W + 10, :] = hr[base + 2, :, lanes].astype(F32)[0:1, :] * keep

    for dr in range(2):
        for dq in range(2):
            at = dr * W + dq
            for h in range(2):
                lo = (2 * dr + dq) * C + h * 128
                x[0:ROWS, lo : lo + 128] = pad[h, at : at + ROWS, :].astype(BF16)

    flat = iota((ROWS, 128), 0)
    t_of = (flat * 6554) >> 16
    u_of = flat - t_of * W
    for i in range(2):
        for j in range(2):
            ph = 2 * i + j
            mixed = jnp.dot(x[0:ROWS, :], wc[:, ph * C : ph * C + C], preferred_element_type=F32)
            at = (1 - i) * W + (1 - j)
            wet = pad[2, at : at + ROWS, :]
            inside = jnp.logical_and(
                jnp.logical_and(t_of >= i, t_of < 64 + i), jnp.logical_and(u_of >= j, u_of < 8 + j)
            )
            for h in range(2):
                m = mixed[:, h * 128 : h * 128 + 128]
                square = m * m
                half = 0.5 + 0.5 * jnp.tanh(m * (GELU_C + (GELU_C * GELU_K) * square))
                slope = half + m * (half * (1.0 - half)) * (
                    2.0 * GELU_C + (6.0 * GELU_C * GELU_K) * square
                )
                spot = pl.ds(1 - j, ROWS, stride=2)
                adj = wet * ct[i, h, spot, :] * slope
                ct[i, h, spot, :] = wet * (m * half)
                lo = ph * C + h * 128
                a_all[0:ROWS, lo : lo + 128] = adj.astype(BF16)
                a_own[0:ROWS, lo : lo + 128] = jnp.where(inside, adj, 0.0).astype(BF16)
            gt[ph] = lax.dot_general(
                a_own[:, ph * C : ph * C + C], x[...], (((0,), (0,)), ((), ())),
                preferred_element_type=F32,
            )

    picks = (((0, 0), (1, 0)), ((0, 1), (1, 0)), ((0, 1), (1, 1)))
    scale = 1.0 / 512.0
    for ka in range(3):
        for kb in range(3):
            for h in range(2):
                total = None
                for i, dr in picks[ka]:
                    for j, dq in picks[kb]:
                        lo = (2 * dr + dq) * C + h * 128
                        term = gt[2 * i + j, :, lo : lo + 128]
                        total = term if total is None else total + term
                total = total * scale
                dw[h, 3 * ka + kb] = total
                sa[h, 3 * ka + kb] = total.astype(BF16)
    move_a = remote(sa.at[1 - core], ra, a_ss.at[0], a_rs.at[0], (a, mate))
    move_a.start()

    z[16 : 16 + ROWS, :] = lax.dot_general(
        a_all[0:ROWS, :], wc[...], (((1,), (1,)), ((), ())), preferred_element_type=F32
    )
    move_a.wait()
    for tap in range(9):
        pair = (dw[core, tap] + ra[tap].astype(F32)).astype(BF16)
        if tap < 5:
            sb[:, tap] = pair.reshape(16, 16, 128)
        else:
            sx[tap - 5] = pair

    def copy_x(k):
        to = lax.rem(a + k, LAT)
        return remote(sx.at[to], rx.at[a], x_ss.at[to], x_rs.at[a], (to, b))

    def recv_x(k):
        fr = lax.rem(a + LAT - k, LAT)
        return remote(sx.at[fr], rx.at[fr], x_ss.at[fr], x_rs.at[fr], (fr, b))

    for k in range(1, LAT):
        copy_x(k).start()
    rx[a] = sx[a]

    def chip_copy(src, dst, ss, rs, k):
        to = lax.rem(chip + k, 16)
        return remote(src.at[to], dst.at[chip], ss.at[to], rs.at[chip], (a, 2 * to + core))

    def chip_recv(src, dst, ss, rs, k):
        fr = lax.rem(chip + 16 - k, 16)
        return remote(src.at[fr], dst.at[fr], ss.at[fr], rs.at[fr], (a, 2 * fr + core))


    total = None
    for dr in range(2):
        for dq in range(2):
            at = 16 - dr * W - dq
            lo = (2 * dr + dq) * C
            term = z[at : at + ROWS, lo : lo + C]
            total = term if total is None else total + term
    cg[0:ROWS, :] = total.astype(BF16)
    sending = jnp.dot(gather_m[...], cg[...], preferred_element_type=F32)
    s3[...] = sending.astype(BF16).reshape(LON, 16, C)
    loop(1, LON, lambda k: lon_copy(s3, r3, s3_ss, s3_rs, k).start())
    r3[b] = s3[b]
    loop(1, 16, lambda k: chip_copy(sb, rb, b_ss, b_rs, k).start())
    rb[chip] = sb[chip]


    target_col = jnp.broadcast_to(target, (128, TOK)).astype(F32).T
    for blk in range(4):
        place_m[0:TOK, blk * 128 : blk * 128 + 128] = one_hot(
            target_col, (iota((TOK, 128), 1) + blk * 128).astype(F32)
        )

    def emit(t, carry):
        for i in range(2):
            at = (t + i) * (2 * W) + 1
            decoded[2 * t + i] = jnp.concatenate(
                [ct[i, 0, pl.ds(at, 16), :], ct[i, 1, pl.ds(at, 16), :]], axis=1
            ).astype(BF16)
        return carry

    lax.fori_loop(0, 64, emit, 0, unroll=4)

    for k in range(1, LAT):
        recv_x(k).wait_recv()
    whole = rx[0].astype(F32)
    for k in range(1, LAT):
        whole = whole + rx[k].astype(F32)
    sy[...] = whole.astype(BF16).reshape(16, 16, 128)
    loop(1, 16, lambda k: chip_copy(sy, ry, y_ss, y_rs, k).start())
    ry[chip] = sy[chip]

    loop(1, LON, lambda k: lon_recv(s3, r3, s3_ss, s3_rs, k).wait_recv())
    back = jnp.dot(perm[1], r3[...].reshape(TOK, C), preferred_element_type=F32)
    s4[...] = back.astype(BF16).reshape(LAT, 128, C)

    def copy4(k):
        to = lax.rem(a + k, LAT)
        return remote(s4.at[to], r4.at[a], s4_ss.at[to], s4_rs.at[a], (to, b))

    def recv4(k):
        fr = lax.rem(a + LAT - k, LAT)
        return remote(s4.at[fr], r4.at[fr], s4_ss.at[fr], s4_rs.at[fr], (fr, b))

    for k in range(1, LAT):
        copy4(k).start()
    r4[a] = s4[a]

    loop(1, 16, lambda k: chip_recv(sb, rb, b_ss, b_rs, k).wait_recv())
    planes = []
    for tap in range(5):
        plane = rb[0, tap].astype(F32)
        for m in range(1, 16):
            plane = plane + rb[m, tap].astype(F32)
        planes.append(plane)
    loop(1, 16, lambda k: chip_recv(sy, ry, y_ss, y_rs, k).wait_recv())
    plane = ry[0].astype(F32)
    for m in range(1, 16):
        plane = plane + ry[m].astype(F32)
    planes.append(plane)
    for c in range(2):
        eight = slice(8 * c, 8 * c + 8)
        for n in range(3):
            sd[c, n] = jnp.concatenate(
                [planes[2 * n][eight, :], planes[2 * n + 1][eight, :]], axis=0
            ).astype(BF16)

    def pair_of(k, c):
        return lax.rem(a + k, LAT), lax.rem(core + c, 2)

    def copy_d(k, c):
        aa, cc = pair_of(k, c)
        return remote(
            sd.at[cc], rd.at[core, a], d_ss.at[cc, aa], d_rs.at[core, a], (aa, 2 * chip + cc)
        )

    def recv_d(k, c):
        aa, cc = pair_of(LAT - k, c)
        return remote(
            sd.at[cc], rd.at[cc, aa], d_ss.at[cc, aa], d_rs.at[cc, aa], (aa, 2 * chip + cc)
        )

    others = [(k, c) for c in range(2) for k in range(LAT) if (k, c) != (0, 0)]
    for k, c in others:
        copy_d(k, c).start()
    rd[core, a] = sd[core]

    for k in range(1, LAT):
        recv4(k).wait_recv()
    tgrad[...] = jnp.dot(
        place_m[0:TOK, :], r4[...].reshape(TOK, C), preferred_element_type=F32
    ).astype(BF16)

    for k, c in others:
        recv_d(k, c).wait_recv()
    for c in range(2):
        lanes = slice(c * 128, c * 128 + 128)
        for n in range(3):
            quad = [rd[c, k, n].astype(F32) for k in range(LAT)]
            total = (quad[0] + quad[1]) + (quad[2] + quad[3])
            wgrad[2 * n, :, lanes] = total[0:8, :]
            if n < 2:
                wgrad[2 * n + 1, :, lanes] = total[8:16, :]
        for k in range(LAT):
            wgrad[5 + k, :, lanes] = quad[k][8:16, :]

    for k in range(1, LAT):
        copy1(k).wait_send()
        copy4(k).wait_send()
    loop(1, LON, lambda k: lon_copy(s2, r2, s2_ss, s2_rs, k).wait_send())
    loop(1, LON, lambda k: lon_copy(s3, r3, s3_ss, s3_rs, k).wait_send())
    for k in range(1, LAT):
        copy_x(k).wait_send()
    loop(1, 16, lambda k: chip_copy(sb, rb, b_ss, b_rs, k).wait_send())
    loop(1, 16, lambda k: chip_copy(sy, ry, y_ss, y_rs, k).wait_send())
    for k, c in others:
        copy_d(k, c).wait_send()


def hand_over_kernel(decoded, wgrad, tgrad, decoded_out, wgrad_out, tgrad_out, sems):
    copies = [
        pltpu.make_async_copy(
            decoded.at[pl.ds(n * 32, 32)], decoded_out.at[pl.ds(n * 32, 32)], sems.at[n]
        )
        for n in range(4)
    ]
    copies.append(pltpu.make_async_copy(wgrad, wgrad_out, sems.at[4]))
    copies.append(pltpu.make_async_copy(tgrad, tgrad_out, sems.at[5]))
    for copy in copies:
        copy.start()
    for copy in copies:
        copy.wait()


def local(tokens, dest_tile, slot_cell, w_up, w_down, w_proj, w_conv, cotangent):
    vmem = pl.BlockSpec(memory_space=pltpu.VMEM)
    hbm = pl.BlockSpec(memory_space=pltpu.HBM)
    dma = pltpu.SemaphoreType.DMA
    v = pltpu.VMEM
    decoded, wgrad, tgrad = pl.pallas_call(
        grid_kernel,
        out_shape=(v((128, 16, C), BF16), v((9, 8, C), F32), v((TOK, C), BF16)),
        in_specs=[hbm] * 8,
        out_specs=(vmem, vmem, vmem),
        scratch_shapes=[
            v((TOK, D), BF16),
            v((RING, D, BLOCK), BF16),
            v((RING, BLOCK, D), BF16),
            v((TOK, D), BF16),
            v((TOK, D), F32),
            v((TOK, BLOCK), F32),
            v((TOK, BLOCK), F32),
            v((1, TOK), jnp.int32),
            v((CAP, 128), jnp.int32),
            v((D, C), BF16),
            v((9, C, C), BF16),
            v((128, 16, C), BF16),
            v((LAT, 128, C), BF16),
            dma((4,)), dma((RING,)), dma((RING,)), dma((5,)),
            v((LAT, 128, C), BF16),
            v((LON, 16, C), BF16),
            v((LON, 16, C), BF16),
            v((4 * C, 4 * C), BF16),
            v((3, 680, 128), F32),
            v((PADDED, 4 * C), BF16),
            v((2, 2, 2 * ROWS, 128), F32),
            v((PADDED, 4 * C), BF16),
            v((PADDED, 4 * C), BF16),
            v((16 + ROWS, 4 * C), F32),
            v((PADDED, C), BF16),
            v((4, C, 4 * C), F32),
            v((2, 9, C, 128), F32),
            v((2, 9, C, 128), BF16),
            v((9, C, 128), BF16),
            v((16, 5, 16, 128), BF16),
            v((16, 5, 16, 128), BF16),
            v((LAT, C, 128), BF16),
            v((LAT, C, 128), BF16),
            v((16, 16, 128), BF16),
            v((16, 16, 128), BF16),
            v((2, 3, 16, 128), BF16),
            v((2, LAT, 3, 16, 128), BF16),
            v((2, TOK, TOK), BF16),
            v((832, TOK), BF16),
            v((TOK, PADDED), BF16),
            v((160, C + 128), BF16),
            v((2, 64, C + 128), BF16),
            v((6, 16, C + 128), BF16),
            v((2, 128, C), BF16),
            v((2, 128, C), BF16),
            v((6, 16, C), BF16),
            v((LON, 16, C), BF16),
            v((LON, 16, C), BF16),
            v((LAT, 128, C), BF16),
            v((LAT, 128, C), BF16),
            dma((LAT,)), dma((LAT,)), dma((LON,)), dma((LON,)), dma((8,)), dma((8,)),
            dma((8,)), dma((8,)), dma((LON,)), dma((LON,)), dma((LAT,)), dma((LAT,)),
            dma((1,)), dma((1,)), dma((16,)), dma((16,)), dma((2, LAT)), dma((2, LAT)),
            dma((LAT,)), dma((LAT,)), dma((16,)), dma((16,)),
        ],
        compiler_params=pltpu.CompilerParams(
            collective_id=0, has_side_effects=True, vmem_limit_bytes=58 * 1024 * 1024
        ),
        cost_estimate=pl.CostEstimate(
            flops=22_000_000_000, bytes_accessed=24_000_000, transcendentals=2_600_000
        ),
        name="grid",
    )(
        tokens, dest_tile.reshape(1, TOK), slot_cell.reshape(LAT * LON, CAP).T, w_up, w_down, w_proj,
        w_conv.reshape(9, C, C), cotangent,
    )
    decoded, wgrad, tgrad = pl.pallas_call(
        hand_over_kernel,
        out_shape=(
            jax.ShapeDtypeStruct((128, 16, C), BF16),
            jax.ShapeDtypeStruct((9, 8, C), F32),
            jax.ShapeDtypeStruct((TOK, C), BF16),
        ),
        in_specs=[vmem] * 3,
        out_specs=(hbm, hbm, hbm),
        scratch_shapes=[dma((6,))],
        compiler_params=pltpu.CompilerParams(vmem_limit_bytes=1024 * 1024),
        name="hand_over",
    )(*(pltpu.with_memory_space_constraint(r, pltpu.VMEM) for r in (decoded, wgrad, tgrad)))
    weight_grad = wgrad.reshape(3, 3, 8, C).transpose(0, 1, 3, 2)
    return decoded, weight_grad, tgrad


def solution(mesh):
    in_specs = (
        P(("lat", "lon"), None),
        P(("lat", "lon")),
        P(("lat", "lon"), None, None),
        P(),
        P(),
        P(),
        P(),
        P("lat", "lon", None),
    )
    out_specs = (P("lat", "lon", None), P(None, None, None, "lon"), P(("lat", "lon"), None))
    return jax.shard_map(local, mesh=mesh, in_specs=in_specs, out_specs=out_specs, check_vma=False)
```

```python
import functools
import math

import jax
import jax.numpy as jnp
from jax import lax
from jax.experimental import pallas as pl
from jax.experimental.pallas import tpu as pltpu
from jax.sharding import PartitionSpec as P

F32 = jnp.float32
BF16 = jnp.bfloat16
MESH = pl.DeviceIdType.MESH

D = 1024
MLP = 4096
C = 256
CAP = 4
TOK = 512
LAT = 4
LON = 32
STEPS = 4
BLOCK = MLP // STEPS
RING = 3

W = 10
ROWS = 656
PADDED = 768
GELU_C = math.sqrt(2.0 / math.pi)
GELU_K = 0.044715


def gelu(x):
    return 0.5 * x * (1.0 + jnp.tanh(x * (GELU_C + (GELU_C * GELU_K) * (x * x))))


def iota(shape, dim):
    return lax.broadcasted_iota(jnp.int32, shape, dim)


def one_hot(left, right):
    return jnp.where(left == right, 1.0, 0.0).astype(BF16)


def grid_kernel(
    tokens_h, dest_h, slot_h, w_up, w_down, w_proj_h, w_conv_h, cot_h,
    decoded, wgrad, tgrad,
    tok_v, up_v, down_v, normed, acc, inner_0, inner_1, dest_v, slot_v, w_proj, w_conv, cot, outgoing,
    tok_sem, up_sem, down_sem, in_sem,
    r1, s2, r2, wc, pad, x, ct, a_all, a_own, z, cg, gt, dw, sa, ra, sb, rb, sx, rx, sy, ry, sd, rd,
    perm, place_m, gather_m, se, hc, hr, cse, chc, chr_,
    s3, r3, s4, r4,
    s1_ss, s1_rs, s2_ss, s2_rs, ch_ss, ch_rs, lh_ss, lh_rs, s3_ss, s3_rs, s4_ss, s4_rs,
    a_ss, a_rs, b_ss, b_rs, d_ss, d_rs, x_ss, x_rs, y_ss, y_rs,
):
    a = lax.axis_index("lat")
    b = lax.axis_index("lon")
    core = lax.rem(b, 2)
    chip = b // 2
    a_up, a_dn = lax.rem(a + LAT - 1, LAT), lax.rem(a + 1, LAT)
    b_lf, b_rt = lax.rem(b + LON - 1, LON), lax.rem(b + 1, LON)
    mate = b + 1 - 2 * core

    def remote(src, dst, ss, rs, dev):
        return pltpu.make_async_remote_copy(
            src_ref=src, dst_ref=dst, send_sem=ss, recv_sem=rs, device_id=dev, device_id_type=MESH
        )

    small = [
        pltpu.make_async_copy(src, dst, in_sem.at[n])
        for n, (src, dst) in enumerate((
            (dest_h, dest_v), (slot_h, slot_v), (w_proj_h, w_proj), (cot_h, cot), (w_conv_h, w_conv)
        ))
    ]
    tok_copies = [
        pltpu.make_async_copy(
            tokens_h.at[pl.ds(n * 128, 128), :], tok_v.at[pl.ds(n * 128, 128), :], tok_sem.at[n]
        )
        for n in range(4)
    ]

    def up_copy(j):
        at = j % RING
        return pltpu.make_async_copy(w_up.at[:, pl.ds(j * BLOCK, BLOCK)], up_v.at[at], up_sem.at[at])

    def down_copy(j):
        at = j % RING
        return pltpu.make_async_copy(w_down.at[pl.ds(j * BLOCK, BLOCK), :], down_v.at[at], down_sem.at[at])

    for copy in tok_copies:
        copy.start()
    up_copy(0).start()
    for n in range(2):
        small[n].start()
    up_copy(1).start()
    down_copy(0).start()
    for n in range(2, RING):
        up_copy(n).start()
        down_copy(n - 1).start()
    down_copy(RING - 1).start()

    barrier = pltpu.get_barrier_semaphore()

    def greet(dev):
        pl.semaphore_signal(barrier, inc=1, device_id=dev, device_id_type=MESH)

    for k in range(1, LAT):
        greet((lax.rem(a + k, LAT), b))

    def greet_lon(k, carry):
        greet((a, lax.rem(b + k, LON)))
        return carry

    lax.fori_loop(1, LON, greet_lon, 0)
    for aa in (a_up, a_dn):
        for bb in (b_lf, b_rt):
            greet((aa, bb))
    for k in range(1, LAT):
        greet((lax.rem(a + k, LAT), mate))

    for copy in small[2:]:
        copy.start()

    small[0].wait()
    small[1].wait()
    dest = jnp.broadcast_to(dest_v[...], (8, TOK))
    place = iota((8, TOK), 1)
    rank = jnp.zeros((8, TOK), jnp.int32)
    for step in range(1, CAP):
        same = jnp.logical_and(pltpu.roll(dest, step, 1) == dest, place >= step)
        rank = rank + jnp.where(same, 1, 0)
    target = jnp.where(dest < LAT * LON, dest * CAP + rank, -2)[:1, :]
    order = iota((128, TOK), 1)
    spread = one_hot(((order >> 2) & 3) * LON + (order >> 4), iota((128, TOK), 0))
    by_rank = slot_v[...]
    spread_of = lambda part: jnp.dot(
        part.astype(F32).astype(BF16), spread, preferred_element_type=F32
    )
    moved = 8.0 * spread_of(by_rank >> 3) + spread_of(by_rank & 7)
    rank_is = (iota((CAP, TOK), 1) & 3) == iota((CAP, TOK), 0)
    slot_row = jnp.sum(jnp.where(rank_is, moved, 0.0), axis=0, keepdims=True).astype(jnp.int32)

    inner = (inner_0, inner_1)
    for n in range(4):
        tok_copies[n].wait()
        rows = slice(n * 128, n * 128 + 128)
        values = tok_v[rows, :].astype(F32)
        center = values - jnp.mean(values, axis=1, keepdims=True)
        variance = jnp.mean(center * center, axis=1, keepdims=True)
        normed[rows, :] = (center * lax.rsqrt(variance + 1e-05)).astype(BF16)
        acc[rows, :] = values
    up_copy(0).wait()
    inner[0][...] = jnp.dot(normed[...], up_v[0], preferred_element_type=F32)

    for j in range(STEPS):
        last = j == STEPS - 1
        if not last:
            up_copy(j + 1).wait()
        down_copy(j).wait()
        hidden = gelu(inner[j % 2][...]).astype(BF16)
        if not last:
            inner[(j + 1) % 2][...] = jnp.dot(
                normed[...], up_v[(j + 1) % RING], preferred_element_type=F32
            )
        acc[...] += jnp.dot(hidden, down_v[j % RING], preferred_element_type=F32)
        if j + RING < STEPS:
            up_copy(j + RING).start()
            down_copy(j + RING).start()
    small[2].wait()
    payload = jnp.dot(acc[...].astype(BF16), w_proj[...], preferred_element_type=F32).astype(BF16)
    selector = one_hot(iota((TOK, TOK), 0), target)
    outgoing[...] = (
        jnp.dot(selector, payload, preferred_element_type=F32).astype(BF16).reshape(LAT, 128, C)
    )
    pl.semaphore_wait(barrier, (LAT - 1) + (LON - 1) + 4 + (LAT - 1))

    def copy1(k):
        to = lax.rem(a + k, LAT)
        return remote(outgoing.at[to], r1.at[a], s1_ss.at[to], s1_rs.at[a], (to, b))

    def recv1(k):
        fr = lax.rem(a + LAT - k, LAT)
        return remote(outgoing.at[fr], r1.at[fr], s1_ss.at[fr], s1_rs.at[fr], (fr, b))

    for k in range(1, LAT):
        copy1(k).start()
    r1[a] = outgoing[a]

    small[3].wait()
    ct[...] = jnp.zeros_like(ct)

    def fill(t, carry):
        even = cot[2 * t].astype(F32)
        odd = cot[2 * t + 1].astype(F32)
        for h in range(2):
            lanes = slice(h * 128, h * 128 + 128)
            ct[0, h, pl.ds(t * (2 * W) + 1, 16), :] = even[:, lanes]
            ct[1, h, pl.ds(t * (2 * W) + (2 * W) + 1, 16), :] = odd[:, lanes]
        return carry

    lax.fori_loop(0, 64, fill, 0, unroll=4)
    for side, col in enumerate((1, 16)):
        for i in range(2):
            for h in range(2):
                cse[side, pl.ds(64 * i, 64), h * 128 : h * 128 + 128] = ct[
                    i, h, pl.ds(i * 2 * W + col, 64, stride=2 * W), :
                ].astype(BF16)

    row_moves = (
        ("bottom", a_dn, b, 0), ("bottom", a_dn, b_rt, 1), ("bottom", a_dn, b_lf, 2),
        ("top", a_up, b, 3), ("top", a_up, b_rt, 4), ("top", a_up, b_lf, 5),
    )

    def halo_copies(cols, rows, col_dst, row_dst, ss, rs):
        moves = [
            remote(cols(1), col_dst.at[0], ss.at[0], rs.at[0], (a, b_rt)),
            remote(cols(0), col_dst.at[1], ss.at[1], rs.at[1], (a, b_lf)),
        ]
        for name, aa, bb, slot in row_moves:
            moves.append(
                remote(rows(name), row_dst.at[slot], ss.at[2 + slot], rs.at[2 + slot], (aa, bb))
            )
        return moves

    cot_moves = halo_copies(
        lambda side: cse.at[side],
        lambda name: cot.at[0] if name == "top" else cot.at[127],
        chc, chr_, ch_ss, ch_rs,
    )
    for move in cot_moves:
        move.start()

    row, col = iota((TOK, TOK), 0), iota((TOK, TOK), 1)
    perm[0] = one_hot(((row >> 2) & 3) * 128 + (row >> 4) * 4 + (row & 3), col)
    perm[1] = one_hot(((col >> 2) & 3) * 128 + (col >> 4) * 4 + (col & 3), row)

    for k in range(1, LAT):
        recv1(k).wait_recv()
    mixed_rows = jnp.dot(perm[0], r1[...].reshape(TOK, C), preferred_element_type=F32)
    s2[...] = mixed_rows.astype(BF16).reshape(LON, 16, C)

    def lon_copy(src, dst, ss, rs, k):
        to = lax.rem(b + k, LON)
        return remote(src.at[to], dst.at[b], ss.at[0], rs.at[0], (a, to))

    def group(src, dst, ss, rs, peers):
        return remote(
            src.at[pl.ds(0, peers)], dst.at[pl.ds(0, peers)], ss.at[0], rs.at[0], (a, b_rt)
        )

    def loop(lo, hi, body):
        def step(k, carry):
            body(k)
            return carry

        lax.fori_loop(lo, hi, step, 0)

    loop(1, LON, lambda k: lon_copy(s2, r2, s2_ss, s2_rs, k).start())
    r2[b] = s2[b]

    small[4].wait()
    combos = {(0, 0): (0,), (1, 0): (1, 2), (0, 1): (0, 1), (1, 1): (2,)}
    for dr in range(2):
        for dq in range(2):
            for i in range(2):
                for j in range(2):
                    total = None
                    for ka in combos[dr, i]:
                        for kb in combos[dq, j]:
                            term = w_conv[3 * ka + kb].astype(F32)
                            total = term if total is None else total + term
                    wc[
                        (2 * dr + dq) * C : (2 * dr + dq + 1) * C, (2 * i + j) * C : (2 * i + j + 1) * C
                    ] = total.astype(BF16)

    slot = jnp.broadcast_to(slot_row, (128, TOK))
    flat_row = jnp.where(slot < TOK, ((slot >> 3) + 1) * W + (slot & 7) + 1, -2)[:1, :]
    place_m[160:832, :] = one_hot(iota((672, TOK), 0), flat_row)
    edge = iota((160, 1), 0)
    cell = jnp.where(
        edge < 64, edge * 8,
        jnp.where(
            edge < 128, (edge - 64) * 8 + 7,
            jnp.where(
                edge < 144, jnp.where(edge < 136, edge - 128, -2),
                jnp.where(edge < 152, edge - 144 + 504, -2),
            ),
        ),
    )
    place_m[0:160, :] = one_hot(cell, slot[:1, :])
    flat_col = jnp.where(slot < TOK, ((slot >> 3) + 1) * W + (slot & 7) + 1, -2).astype(F32).T
    for blk in range(PADDED // 128):
        gather_m[:, blk * 128 : blk * 128 + 128] = one_hot(
            flat_col, (iota((TOK, 128), 1) + blk * 128).astype(F32)
        )
    x[ROWS:, :] = jnp.zeros((PADDED - ROWS, 4 * C), BF16)
    a_own[ROWS:, :] = jnp.zeros((PADDED - ROWS, 4 * C), BF16)
    cg[ROWS:, :] = jnp.zeros((PADDED - ROWS, C), BF16)
    z[0:16, :] = jnp.zeros((16, 4 * C), F32)
    pad[:, 672:, :] = jnp.zeros((3, 8, 128), F32)

    keep_top = jnp.where(a > 0, 1.0, 0.0)
    keep_bot = jnp.where(a < LAT - 1, 1.0, 0.0)

    for move in cot_moves:
        move.wait()
    for h in range(2):
        lanes = slice(h * 128, h * 128 + 128)
        for i in range(2):
            for side, at in ((0, 0), (1, 17)):
                ct[i, h, pl.ds(i * 2 * W + at, 64, stride=2 * W), :] = chc[
                    side, pl.ds(64 * i, 64), lanes
                ].astype(F32)
        for base, i, t, keep in ((0, 1, 0, keep_top), (3, 0, 64, keep_bot)):
            ct[i, h, t * 2 * W + 1 : t * 2 * W + 17, :] = chr_[base, :, lanes].astype(F32) * keep
            ct[i, h, t * 2 * W : t * 2 * W + 1, :] = (
                chr_[base + 1, :, lanes].astype(F32)[15:16, :] * keep
            )
            ct[i, h, t * 2 * W + 17 : t * 2 * W + 18, :] = (
                chr_[base + 2, :, lanes].astype(F32)[0:1, :] * keep
            )

    group(s2, r2, s2_ss, s2_rs, LON - 1).wait_recv()
    arrived = jnp.concatenate(
        [r2[...].reshape(TOK, C), jnp.ones((TOK, 128), BF16)], axis=1
    )
    se[...] = jnp.dot(place_m[0:160, :], arrived, preferred_element_type=F32).astype(BF16)
    lat_moves = halo_copies(
        lambda side: se.at[pl.ds(64 * side, 64)],
        lambda name: se.at[pl.ds(128, 16)] if name == "top" else se.at[pl.ds(144, 16)],
        hc, hr, lh_ss, lh_rs,
    )
    for move in lat_moves:
        move.start()
    placed = jnp.dot(place_m[160:832, :], arrived, preferred_element_type=F32)
    for lane in range(3):
        pad[lane, 0:672, :] = placed[:, lane * 128 : lane * 128 + 128]
    for move in lat_moves:
        move.wait()
    for lane in range(3):
        lanes = slice(lane * 128, lane * 128 + 128)
        for side, at in ((0, 0), (1, W - 1)):
            pad[lane, pl.ds(W + at, 64, stride=W), :] = hc[side, :, lanes].astype(F32)
        for base, t, keep in ((0, 0, keep_top), (3, 65, keep_bot)):
            pad[lane, t * W + 1 : t * W + 9, :] = hr[base, :, lanes].astype(F32)[0:8, :] * keep
            pad[lane, t * W : t * W + 1, :] = hr[base + 1, :, lanes].astype(F32)[7:8, :] * keep
            pad[lane, t * W + 9 : t * W + 10, :] = hr[base + 2, :, lanes].astype(F32)[0:1, :] * keep

    for dr in range(2):
        for dq in range(2):
            at = dr * W + dq
            for h in range(2):
                lo = (2 * dr + dq) * C + h * 128
                x[0:ROWS, lo : lo + 128] = pad[h, at : at + ROWS, :].astype(BF16)

    flat = iota((ROWS, 128), 0)
    t_of = (flat * 6554) >> 16
    u_of = flat - t_of * W
    for i in range(2):
        for j in range(2):
            ph = 2 * i + j
            mixed = jnp.dot(x[0:ROWS, :], wc[:, ph * C : ph * C + C], preferred_element_type=F32)
            at = (1 - i) * W + (1 - j)
            wet = pad[2, at : at + ROWS, :]
            inside = jnp.logical_and(
                jnp.logical_and(t_of >= i, t_of < 64 + i), jnp.logical_and(u_of >= j, u_of < 8 + j)
            )
            for h in range(2):
                m = mixed[:, h * 128 : h * 128 + 128]
                square = m * m
                half = 0.5 + 0.5 * jnp.tanh(m * (GELU_C + (GELU_C * GELU_K) * square))
                slope = half + m * (half * (1.0 - half)) * (
                    2.0 * GELU_C + (6.0 * GELU_C * GELU_K) * square
                )
                spot = pl.ds(1 - j, ROWS, stride=2)
                adj = wet * ct[i, h, spot, :] * slope
                ct[i, h, spot, :] = wet * (m * half)
                lo = ph * C + h * 128
                a_all[0:ROWS, lo : lo + 128] = adj.astype(BF16)
                a_own[0:ROWS, lo : lo + 128] = jnp.where(inside, adj, 0.0).astype(BF16)
            gt[ph] = lax.dot_general(
                a_own[:, ph * C : ph * C + C], x[...], (((0,), (0,)), ((), ())),
                preferred_element_type=F32,
            )

    picks = (((0, 0), (1, 0)), ((0, 1), (1, 0)), ((0, 1), (1, 1)))
    scale = 1.0 / 512.0
    for ka in range(3):
        for kb in range(3):
            for h in range(2):
                total = None
                for i, dr in picks[ka]:
                    for j, dq in picks[kb]:
                        lo = (2 * dr + dq) * C + h * 128
                        term = gt[2 * i + j, :, lo : lo + 128]
                        total = term if total is None else total + term
                total = total * scale
                dw[h, 3 * ka + kb] = total
                sa[h, 3 * ka + kb] = total.astype(BF16)
    move_a = remote(sa.at[1 - core], ra, a_ss.at[0], a_rs.at[0], (a, mate))
    move_a.start()

    z[16 : 16 + ROWS, :] = lax.dot_general(
        a_all[0:ROWS, :], wc[...], (((1,), (1,)), ((), ())), preferred_element_type=F32
    )
    move_a.wait()
    for tap in range(9):
        pair = (dw[core, tap] + ra[tap].astype(F32)).astype(BF16)
        if tap < 5:
            sb[:, tap] = pair.reshape(16, 16, 128)
        else:
            sx[tap - 5] = pair

    def copy_x(k):
        to = lax.rem(a + k, LAT)
        return remote(sx.at[to], rx.at[a], x_ss.at[to], x_rs.at[a], (to, b))

    def recv_x(k):
        fr = lax.rem(a + LAT - k, LAT)
        return remote(sx.at[fr], rx.at[fr], x_ss.at[fr], x_rs.at[fr], (fr, b))

    for k in range(1, LAT):
        copy_x(k).start()
    rx[a] = sx[a]

    def chip_copy(src, dst, ss, rs, k):
        to = lax.rem(chip + k, 16)
        return remote(src.at[to], dst.at[chip], ss.at[0], rs.at[0], (a, 2 * to + core))

    total = None
    for dr in range(2):
        for dq in range(2):
            at = 16 - dr * W - dq
            lo = (2 * dr + dq) * C
            term = z[at : at + ROWS, lo : lo + C]
            total = term if total is None else total + term
    cg[0:ROWS, :] = total.astype(BF16)
    sending = jnp.dot(gather_m[...], cg[...], preferred_element_type=F32)
    s3[...] = sending.astype(BF16).reshape(LON, 16, C)
    loop(1, LON, lambda k: lon_copy(s3, r3, s3_ss, s3_rs, k).start())
    r3[b] = s3[b]
    loop(1, 16, lambda k: chip_copy(sb, rb, b_ss, b_rs, k).start())
    rb[chip] = sb[chip]


    target_col = jnp.broadcast_to(target, (128, TOK)).astype(F32).T
    for blk in range(4):
        place_m[0:TOK, blk * 128 : blk * 128 + 128] = one_hot(
            target_col, (iota((TOK, 128), 1) + blk * 128).astype(F32)
        )

    def emit(t, carry):
        for i in range(2):
            at = (t + i) * (2 * W) + 1
            decoded[2 * t + i] = jnp.concatenate(
                [ct[i, 0, pl.ds(at, 16), :], ct[i, 1, pl.ds(at, 16), :]], axis=1
            ).astype(BF16)
        return carry

    lax.fori_loop(0, 64, emit, 0, unroll=4)

    for k in range(1, LAT):
        recv_x(k).wait_recv()
    whole = rx[0].astype(F32)
    for k in range(1, LAT):
        whole = whole + rx[k].astype(F32)
    sy[...] = whole.astype(BF16).reshape(16, 16, 128)
    loop(1, 16, lambda k: chip_copy(sy, ry, y_ss, y_rs, k).start())
    ry[chip] = sy[chip]

    group(s3, r3, s3_ss, s3_rs, LON - 1).wait_recv()
    back = jnp.dot(perm[1], r3[...].reshape(TOK, C), preferred_element_type=F32)
    s4[...] = back.astype(BF16).reshape(LAT, 128, C)

    def copy4(k):
        to = lax.rem(a + k, LAT)
        return remote(s4.at[to], r4.at[a], s4_ss.at[to], s4_rs.at[a], (to, b))

    def recv4(k):
        fr = lax.rem(a + LAT - k, LAT)
        return remote(s4.at[fr], r4.at[fr], s4_ss.at[fr], s4_rs.at[fr], (fr, b))

    for k in range(1, LAT):
        copy4(k).start()
    r4[a] = s4[a]

    group(sb, rb, b_ss, b_rs, 15).wait_recv()
    planes = []
    for tap in range(5):
        plane = rb[0, tap].astype(F32)
        for m in range(1, 16):
            plane = plane + rb[m, tap].astype(F32)
        planes.append(plane)
    group(sy, ry, y_ss, y_rs, 15).wait_recv()
    plane = ry[0].astype(F32)
    for m in range(1, 16):
        plane = plane + ry[m].astype(F32)
    planes.append(plane)
    for c in range(2):
        eight = slice(8 * c, 8 * c + 8)
        for n in range(3):
            sd[c, n] = jnp.concatenate(
                [planes[2 * n][eight, :], planes[2 * n + 1][eight, :]], axis=0
            ).astype(BF16)

    def pair_of(k, c):
        return lax.rem(a + k, LAT), lax.rem(core + c, 2)

    def copy_d(k, c):
        aa, cc = pair_of(k, c)
        return remote(
            sd.at[cc], rd.at[core, a], d_ss.at[cc, aa], d_rs.at[core, a], (aa, 2 * chip + cc)
        )

    def recv_d(k, c):
        aa, cc = pair_of(LAT - k, c)
        return remote(
            sd.at[cc], rd.at[cc, aa], d_ss.at[cc, aa], d_rs.at[cc, aa], (aa, 2 * chip + cc)
        )

    others = [(k, c) for c in range(2) for k in range(LAT) if (k, c) != (0, 0)]
    for k, c in others:
        copy_d(k, c).start()
    rd[core, a] = sd[core]

    for k in range(1, LAT):
        recv4(k).wait_recv()
    tgrad[...] = jnp.dot(
        place_m[0:TOK, :], r4[...].reshape(TOK, C), preferred_element_type=F32
    ).astype(BF16)

    for k, c in others:
        recv_d(k, c).wait_recv()
    for c in range(2):
        lanes = slice(c * 128, c * 128 + 128)
        for n in range(3):
            quad = [rd[c, k, n].astype(F32) for k in range(LAT)]
            total = (quad[0] + quad[1]) + (quad[2] + quad[3])
            wgrad[2 * n, :, lanes] = total[0:8, :]
            if n < 2:
                wgrad[2 * n + 1, :, lanes] = total[8:16, :]
        for k in range(LAT):
            wgrad[5 + k, :, lanes] = quad[k][8:16, :]

    for k in range(1, LAT):
        copy1(k).wait_send()
        copy4(k).wait_send()
    group(s2, r2, s2_ss, s2_rs, LON - 1).wait_send()
    group(s3, r3, s3_ss, s3_rs, LON - 1).wait_send()
    for k in range(1, LAT):
        copy_x(k).wait_send()
    group(sb, rb, b_ss, b_rs, 15).wait_send()
    group(sy, ry, y_ss, y_rs, 15).wait_send()
    for k, c in others:
        copy_d(k, c).wait_send()


def hand_over_kernel(decoded, wgrad, tgrad, decoded_out, wgrad_out, tgrad_out, sems):
    copies = [
        pltpu.make_async_copy(
            decoded.at[pl.ds(n * 32, 32)], decoded_out.at[pl.ds(n * 32, 32)], sems.at[n]
        )
        for n in range(4)
    ]
    copies.append(pltpu.make_async_copy(wgrad, wgrad_out, sems.at[4]))
    copies.append(pltpu.make_async_copy(tgrad, tgrad_out, sems.at[5]))
    for copy in copies:
        copy.start()
    for copy in copies:
        copy.wait()


def local(tokens, dest_tile, slot_cell, w_up, w_down, w_proj, w_conv, cotangent):
    vmem = pl.BlockSpec(memory_space=pltpu.VMEM)
    hbm = pl.BlockSpec(memory_space=pltpu.HBM)
    dma = pltpu.SemaphoreType.DMA
    v = pltpu.VMEM
    decoded, wgrad, tgrad = pl.pallas_call(
        grid_kernel,
        out_shape=(v((128, 16, C), BF16), v((9, 8, C), F32), v((TOK, C), BF16)),
        in_specs=[hbm] * 8,
        out_specs=(vmem, vmem, vmem),
        scratch_shapes=[
            v((TOK, D), BF16),
            v((RING, D, BLOCK), BF16),
            v((RING, BLOCK, D), BF16),
            v((TOK, D), BF16),
            v((TOK, D), F32),
            v((TOK, BLOCK), F32),
            v((TOK, BLOCK), F32),
            v((1, TOK), jnp.int32),
            v((CAP, 128), jnp.int32),
            v((D, C), BF16),
            v((9, C, C), BF16),
            v((128, 16, C), BF16),
            v((LAT, 128, C), BF16),
            dma((4,)), dma((RING,)), dma((RING,)), dma((5,)),
            v((LAT, 128, C), BF16),
            v((LON, 16, C), BF16),
            v((LON, 16, C), BF16),
            v((4 * C, 4 * C), BF16),
            v((3, 680, 128), F32),
            v((PADDED, 4 * C), BF16),
            v((2, 2, 2 * ROWS, 128), F32),
            v((PADDED, 4 * C), BF16),
            v((PADDED, 4 * C), BF16),
            v((16 + ROWS, 4 * C), F32),
            v((PADDED, C), BF16),
            v((4, C, 4 * C), F32),
            v((2, 9, C, 128), F32),
            v((2, 9, C, 128), BF16),
            v((9, C, 128), BF16),
            v((16, 5, 16, 128), BF16),
            v((16, 5, 16, 128), BF16),
            v((LAT, C, 128), BF16),
            v((LAT, C, 128), BF16),
            v((16, 16, 128), BF16),
            v((16, 16, 128), BF16),
            v((2, 3, 16, 128), BF16),
            v((2, LAT, 3, 16, 128), BF16),
            v((2, TOK, TOK), BF16),
            v((832, TOK), BF16),
            v((TOK, PADDED), BF16),
            v((160, C + 128), BF16),
            v((2, 64, C + 128), BF16),
            v((6, 16, C + 128), BF16),
            v((2, 128, C), BF16),
            v((2, 128, C), BF16),
            v((6, 16, C), BF16),
            v((LON, 16, C), BF16),
            v((LON, 16, C), BF16),
            v((LAT, 128, C), BF16),
            v((LAT, 128, C), BF16),
            dma((LAT,)), dma((LAT,)), dma((LON,)), dma((LON,)), dma((8,)), dma((8,)),
            dma((8,)), dma((8,)), dma((LON,)), dma((LON,)), dma((LAT,)), dma((LAT,)),
            dma((1,)), dma((1,)), dma((16,)), dma((16,)), dma((2, LAT)), dma((2, LAT)),
            dma((LAT,)), dma((LAT,)), dma((16,)), dma((16,)),
        ],
        compiler_params=pltpu.CompilerParams(
            collective_id=0, has_side_effects=True, vmem_limit_bytes=58 * 1024 * 1024
        ),
        cost_estimate=pl.CostEstimate(
            flops=22_000_000_000, bytes_accessed=24_000_000, transcendentals=2_600_000
        ),
        name="grid",
    )(
        tokens, dest_tile.reshape(1, TOK), slot_cell.reshape(LAT * LON, CAP).T, w_up, w_down, w_proj,
        w_conv.reshape(9, C, C), cotangent,
    )
    decoded, wgrad, tgrad = pl.pallas_call(
        hand_over_kernel,
        out_shape=(
            jax.ShapeDtypeStruct((128, 16, C), BF16),
            jax.ShapeDtypeStruct((9, 8, C), F32),
            jax.ShapeDtypeStruct((TOK, C), BF16),
        ),
        in_specs=[vmem] * 3,
        out_specs=(hbm, hbm, hbm),
        scratch_shapes=[dma((6,))],
        compiler_params=pltpu.CompilerParams(vmem_limit_bytes=1024 * 1024),
        name="hand_over",
    )(*(pltpu.with_memory_space_constraint(r, pltpu.VMEM) for r in (decoded, wgrad, tgrad)))
    weight_grad = wgrad.reshape(3, 3, 8, C).transpose(0, 1, 3, 2)
    return decoded, weight_grad, tgrad


def solution(mesh):
    in_specs = (
        P(("lat", "lon"), None),
        P(("lat", "lon")),
        P(("lat", "lon"), None, None),
        P(),
        P(),
        P(),
        P(),
        P("lat", "lon", None),
    )
    out_specs = (P("lat", "lon", None), P(None, None, None, "lon"), P(("lat", "lon"), None))
    return jax.shard_map(local, mesh=mesh, in_specs=in_specs, out_specs=out_specs, check_vma=False)
```

```python
import functools
import math

import jax
import jax.numpy as jnp
from jax import lax
from jax.experimental import pallas as pl
from jax.experimental.pallas import tpu as pltpu
from jax.sharding import PartitionSpec as P

F32 = jnp.float32
BF16 = jnp.bfloat16
MESH = pl.DeviceIdType.MESH

D = 1024
MLP = 4096
C = 256
CAP = 4
TOK = 512
LAT = 4
LON = 32
STEPS = 4
BLOCK = MLP // STEPS
RING = 3

W = 10
ROWS = 656
PADDED = 768
GELU_C = math.sqrt(2.0 / math.pi)
GELU_K = 0.044715


def gelu(x):
    return 0.5 * x * (1.0 + jnp.tanh(x * (GELU_C + (GELU_C * GELU_K) * (x * x))))


def iota(shape, dim):
    return lax.broadcasted_iota(jnp.int32, shape, dim)


def one_hot(left, right):
    return jnp.where(left == right, 1.0, 0.0).astype(BF16)


def grid_kernel(
    tokens_h, dest_h, slot_h, w_up, w_down, w_proj_h, w_conv_h, cot_h,
    decoded, wgrad, tgrad,
    tok_v, up_v, down_v, normed, acc, inner_0, inner_1, dest_v, slot_v, w_proj, w_conv, cot, outgoing,
    tok_sem, up_sem, down_sem, in_sem,
    r1, s2, r2, wc, pad, x, ct, a_all, a_own, z, cg, gt, dw, sa, ra, sb, rb, sx, rx, sy, ry, sd, rd,
    perm, place_m, gather_m, se, hc, hr, cse, chc, chr_,
    s3, r3, s4, r4,
    s1_ss, s1_rs, s2_ss, s2_rs, ch_ss, ch_rs, lh_ss, lh_rs, s3_ss, s3_rs, s4_ss, s4_rs,
    a_ss, a_rs, b_ss, b_rs, d_ss, d_rs, x_ss, x_rs, y_ss, y_rs,
):
    a = lax.axis_index("lat")
    b = lax.axis_index("lon")
    core = lax.rem(b, 2)
    chip = b // 2
    a_up, a_dn = lax.rem(a + LAT - 1, LAT), lax.rem(a + 1, LAT)
    b_lf, b_rt = lax.rem(b + LON - 1, LON), lax.rem(b + 1, LON)
    mate = b + 1 - 2 * core

    def remote(src, dst, ss, rs, dev):
        return pltpu.make_async_remote_copy(
            src_ref=src, dst_ref=dst, send_sem=ss, recv_sem=rs, device_id=dev, device_id_type=MESH
        )

    small = [
        pltpu.make_async_copy(src, dst, in_sem.at[n])
        for n, (src, dst) in enumerate((
            (dest_h, dest_v), (slot_h, slot_v), (w_proj_h, w_proj), (cot_h, cot), (w_conv_h, w_conv)
        ))
    ]
    tok_copies = [
        pltpu.make_async_copy(
            tokens_h.at[pl.ds(n * 128, 128), :], tok_v.at[pl.ds(n * 128, 128), :], tok_sem.at[n]
        )
        for n in range(4)
    ]

    def up_copy(j):
        at = j % RING
        return pltpu.make_async_copy(w_up.at[:, pl.ds(j * BLOCK, BLOCK)], up_v.at[at], up_sem.at[at])

    def down_copy(j):
        at = j % RING
        return pltpu.make_async_copy(w_down.at[pl.ds(j * BLOCK, BLOCK), :], down_v.at[at], down_sem.at[at])

    for copy in tok_copies:
        copy.start()
    up_copy(0).start()
    for n in range(2):
        small[n].start()

    barrier = pltpu.get_barrier_semaphore()

    def greet(dev):
        pl.semaphore_signal(barrier, inc=1, device_id=dev, device_id_type=MESH)

    for k in range(1, LAT):
        greet((lax.rem(a + k, LAT), b))

    def greet_lon(k, carry):
        greet((a, lax.rem(b + k, LON)))
        return carry

    lax.fori_loop(1, LON, greet_lon, 0)
    for aa in (a_up, a_dn):
        for bb in (b_lf, b_rt):
            greet((aa, bb))
    for k in range(1, LAT):
        greet((lax.rem(a + k, LAT), mate))

    down_copy(0).start()
    up_copy(1).start()

    small[0].wait()
    small[1].wait()
    dest = jnp.broadcast_to(dest_v[...], (8, TOK))
    place = iota((8, TOK), 1)
    rank = jnp.zeros((8, TOK), jnp.int32)
    for step in range(1, CAP):
        same = jnp.logical_and(pltpu.roll(dest, step, 1) == dest, place >= step)
        rank = rank + jnp.where(same, 1, 0)
    target = jnp.where(dest < LAT * LON, dest * CAP + rank, -2)[:1, :]
    order = iota((128, TOK), 1)
    spread = one_hot(((order >> 2) & 3) * LON + (order >> 4), iota((128, TOK), 0))
    by_rank = slot_v[...]
    spread_of = lambda part: jnp.dot(
        part.astype(F32).astype(BF16), spread, preferred_element_type=F32
    )
    moved = 8.0 * spread_of(by_rank >> 3) + spread_of(by_rank & 7)
    rank_is = (iota((CAP, TOK), 1) & 3) == iota((CAP, TOK), 0)
    slot_row = jnp.sum(jnp.where(rank_is, moved, 0.0), axis=0, keepdims=True).astype(jnp.int32)

    inner = (inner_0, inner_1)
    for n in range(4):
        tok_copies[n].wait()
        rows = slice(n * 128, n * 128 + 128)
        values = tok_v[rows, :].astype(F32)
        center = values - jnp.mean(values, axis=1, keepdims=True)
        variance = jnp.mean(center * center, axis=1, keepdims=True)
        normed[rows, :] = (center * lax.rsqrt(variance + 1e-05)).astype(BF16)
        acc[rows, :] = values
    for n in range(2, RING):
        down_copy(n - 1).start()
        up_copy(n).start()
    down_copy(RING - 1).start()
    up_copy(0).wait()
    inner[0][...] = jnp.dot(normed[...], up_v[0], preferred_element_type=F32)

    for j in range(STEPS):
        last = j == STEPS - 1
        if not last:
            up_copy(j + 1).wait()
        down_copy(j).wait()
        hidden = gelu(inner[j % 2][...]).astype(BF16)
        if not last:
            inner[(j + 1) % 2][...] = jnp.dot(
                normed[...], up_v[(j + 1) % RING], preferred_element_type=F32
            )
        acc[...] += jnp.dot(hidden, down_v[j % RING], preferred_element_type=F32)
        if j + RING < STEPS:
            up_copy(j + RING).start()
            down_copy(j + RING).start()
        if j == 0:
            for copy in small[2:]:
                copy.start()
    small[2].wait()
    payload = jnp.dot(acc[...].astype(BF16), w_proj[...], preferred_element_type=F32).astype(BF16)
    selector = one_hot(iota((TOK, TOK), 0), target)
    outgoing[...] = (
        jnp.dot(selector, payload, preferred_element_type=F32).astype(BF16).reshape(LAT, 128, C)
    )
    pl.semaphore_wait(barrier, (LAT - 1) + (LON - 1) + 4 + (LAT - 1))

    def copy1(k):
        to = lax.rem(a + k, LAT)
        return remote(outgoing.at[to], r1.at[a], s1_ss.at[to], s1_rs.at[a], (to, b))

    def recv1(k):
        fr = lax.rem(a + LAT - k, LAT)
        return remote(outgoing.at[fr], r1.at[fr], s1_ss.at[fr], s1_rs.at[fr], (fr, b))

    for k in range(1, LAT):
        copy1(k).start()
    r1[a] = outgoing[a]

    small[3].wait()
    ct[...] = jnp.zeros_like(ct)

    def fill(t, carry):
        even = cot[2 * t].astype(F32)
        odd = cot[2 * t + 1].astype(F32)
        for h in range(2):
            lanes = slice(h * 128, h * 128 + 128)
            ct[0, h, pl.ds(t * (2 * W) + 1, 16), :] = even[:, lanes]
            ct[1, h, pl.ds(t * (2 * W) + (2 * W) + 1, 16), :] = odd[:, lanes]
        return carry

    lax.fori_loop(0, 64, fill, 0, unroll=4)
    for side, col in enumerate((1, 16)):
        for i in range(2):
            for h in range(2):
                cse[side, pl.ds(64 * i, 64), h * 128 : h * 128 + 128] = ct[
                    i, h, pl.ds(i * 2 * W + col, 64, stride=2 * W), :
                ].astype(BF16)

    row_moves = (
        ("bottom", a_dn, b, 0), ("bottom", a_dn, b_rt, 1), ("bottom", a_dn, b_lf, 2),
        ("top", a_up, b, 3), ("top", a_up, b_rt, 4), ("top", a_up, b_lf, 5),
    )

    def halo_copies(cols, rows, col_dst, row_dst, ss, rs):
        moves = [
            remote(cols(1), col_dst.at[0], ss.at[0], rs.at[0], (a, b_rt)),
            remote(cols(0), col_dst.at[1], ss.at[1], rs.at[1], (a, b_lf)),
        ]
        for name, aa, bb, slot in row_moves:
            moves.append(
                remote(rows(name), row_dst.at[slot], ss.at[2 + slot], rs.at[2 + slot], (aa, bb))
            )
        return moves

    cot_moves = halo_copies(
        lambda side: cse.at[side],
        lambda name: cot.at[0] if name == "top" else cot.at[127],
        chc, chr_, ch_ss, ch_rs,
    )
    for move in cot_moves:
        move.start()

    row, col = iota((TOK, TOK), 0), iota((TOK, TOK), 1)
    perm[0] = one_hot(((row >> 2) & 3) * 128 + (row >> 4) * 4 + (row & 3), col)
    perm[1] = one_hot(((col >> 2) & 3) * 128 + (col >> 4) * 4 + (col & 3), row)

    for k in range(1, LAT):
        recv1(k).wait_recv()
    mixed_rows = jnp.dot(perm[0], r1[...].reshape(TOK, C), preferred_element_type=F32)
    s2[...] = mixed_rows.astype(BF16).reshape(LON, 16, C)

    def lon_copy(src, dst, ss, rs, k):
        to = lax.rem(b + k, LON)
        return remote(src.at[to], dst.at[b], ss.at[0], rs.at[0], (a, to))

    def group(src, dst, ss, rs, peers):
        return remote(
            src.at[pl.ds(0, peers)], dst.at[pl.ds(0, peers)], ss.at[0], rs.at[0], (a, b_rt)
        )

    def loop(lo, hi, body):
        def step(k, carry):
            body(k)
            return carry

        lax.fori_loop(lo, hi, step, 0)

    loop(1, LON, lambda k: lon_copy(s2, r2, s2_ss, s2_rs, k).start())
    r2[b] = s2[b]

    small[4].wait()
    combos = {(0, 0): (0,), (1, 0): (1, 2), (0, 1): (0, 1), (1, 1): (2,)}
    for dr in range(2):
        for dq in range(2):
            for i in range(2):
                for j in range(2):
                    total = None
                    for ka in combos[dr, i]:
                        for kb in combos[dq, j]:
                            term = w_conv[3 * ka + kb].astype(F32)
                            total = term if total is None else total + term
                    wc[
                        (2 * dr + dq) * C : (2 * dr + dq + 1) * C, (2 * i + j) * C : (2 * i + j + 1) * C
                    ] = total.astype(BF16)

    slot = jnp.broadcast_to(slot_row, (128, TOK))
    flat_row = jnp.where(slot < TOK, ((slot >> 3) + 1) * W + (slot & 7) + 1, -2)[:1, :]
    place_m[160:832, :] = one_hot(iota((672, TOK), 0), flat_row)
    edge = iota((160, 1), 0)
    cell = jnp.where(
        edge < 64, edge * 8,
        jnp.where(
            edge < 128, (edge - 64) * 8 + 7,
            jnp.where(
                edge < 144, jnp.where(edge < 136, edge - 128, -2),
                jnp.where(edge < 152, edge - 144 + 504, -2),
            ),
        ),
    )
    place_m[0:160, :] = one_hot(cell, slot[:1, :])
    flat_col = jnp.where(slot < TOK, ((slot >> 3) + 1) * W + (slot & 7) + 1, -2).astype(F32).T
    for blk in range(PADDED // 128):
        gather_m[:, blk * 128 : blk * 128 + 128] = one_hot(
            flat_col, (iota((TOK, 128), 1) + blk * 128).astype(F32)
        )
    x[ROWS:, :] = jnp.zeros((PADDED - ROWS, 4 * C), BF16)
    a_own[ROWS:, :] = jnp.zeros((PADDED - ROWS, 4 * C), BF16)
    cg[ROWS:, :] = jnp.zeros((PADDED - ROWS, C), BF16)
    z[0:16, :] = jnp.zeros((16, 4 * C), F32)
    pad[:, 672:, :] = jnp.zeros((3, 8, 128), F32)

    keep_top = jnp.where(a > 0, 1.0, 0.0)
    keep_bot = jnp.where(a < LAT - 1, 1.0, 0.0)

    for move in cot_moves:
        move.wait()
    for h in range(2):
        lanes = slice(h * 128, h * 128 + 128)
        for i in range(2):
            for side, at in ((0, 0), (1, 17)):
                ct[i, h, pl.ds(i * 2 * W + at, 64, stride=2 * W), :] = chc[
                    side, pl.ds(64 * i, 64), lanes
                ].astype(F32)
        for base, i, t, keep in ((0, 1, 0, keep_top), (3, 0, 64, keep_bot)):
            ct[i, h, t * 2 * W + 1 : t * 2 * W + 17, :] = chr_[base, :, lanes].astype(F32) * keep
            ct[i, h, t * 2 * W : t * 2 * W + 1, :] = (
                chr_[base + 1, :, lanes].astype(F32)[15:16, :] * keep
            )
            ct[i, h, t * 2 * W + 17 : t * 2 * W + 18, :] = (
                chr_[base + 2, :, lanes].astype(F32)[0:1, :] * keep
            )

    group(s2, r2, s2_ss, s2_rs, LON - 1).wait_recv()
    arrived = jnp.concatenate(
        [r2[...].reshape(TOK, C), jnp.ones((TOK, 128), BF16)], axis=1
    )
    se[...] = jnp.dot(place_m[0:160, :], arrived, preferred_element_type=F32).astype(BF16)
    lat_moves = halo_copies(
        lambda side: se.at[pl.ds(64 * side, 64)],
        lambda name: se.at[pl.ds(128, 16)] if name == "top" else se.at[pl.ds(144, 16)],
        hc, hr, lh_ss, lh_rs,
    )
    for move in lat_moves:
        move.start()
    placed = jnp.dot(place_m[160:832, :], arrived, preferred_element_type=F32)
    for lane in range(3):
        pad[lane, 0:672, :] = placed[:, lane * 128 : lane * 128 + 128]
    for move in lat_moves:
        move.wait()
    for lane in range(3):
        lanes = slice(lane * 128, lane * 128 + 128)
        for side, at in ((0, 0), (1, W - 1)):
            pad[lane, pl.ds(W + at, 64, stride=W), :] = hc[side, :, lanes].astype(F32)
        for base, t, keep in ((0, 0, keep_top), (3, 65, keep_bot)):
            pad[lane, t * W + 1 : t * W + 9, :] = hr[base, :, lanes].astype(F32)[0:8, :] * keep
            pad[lane, t * W : t * W + 1, :] = hr[base + 1, :, lanes].astype(F32)[7:8, :] * keep
            pad[lane, t * W + 9 : t * W + 10, :] = hr[base + 2, :, lanes].astype(F32)[0:1, :] * keep

    for dr in range(2):
        for dq in range(2):
            at = dr * W + dq
            for h in range(2):
                lo = (2 * dr + dq) * C + h * 128
                x[0:ROWS, lo : lo + 128] = pad[h, at : at + ROWS, :].astype(BF16)

    flat = iota((ROWS, 128), 0)
    t_of = (flat * 6554) >> 16
    u_of = flat - t_of * W
    for i in range(2):
        for j in range(2):
            ph = 2 * i + j
            mixed = jnp.dot(x[0:ROWS, :], wc[:, ph * C : ph * C + C], preferred_element_type=F32)
            at = (1 - i) * W + (1 - j)
            wet = pad[2, at : at + ROWS, :]
            inside = jnp.logical_and(
                jnp.logical_and(t_of >= i, t_of < 64 + i), jnp.logical_and(u_of >= j, u_of < 8 + j)
            )
            for h in range(2):
                m = mixed[:, h * 128 : h * 128 + 128]
                square = m * m
                half = 0.5 + 0.5 * jnp.tanh(m * (GELU_C + (GELU_C * GELU_K) * square))
                slope = half + m * (half * (1.0 - half)) * (
                    2.0 * GELU_C + (6.0 * GELU_C * GELU_K) * square
                )
                spot = pl.ds(1 - j, ROWS, stride=2)
                adj = wet * ct[i, h, spot, :] * slope
                ct[i, h, spot, :] = wet * (m * half)
                lo = ph * C + h * 128
                a_all[0:ROWS, lo : lo + 128] = adj.astype(BF16)
                a_own[0:ROWS, lo : lo + 128] = jnp.where(inside, adj, 0.0).astype(BF16)
            gt[ph] = lax.dot_general(
                a_own[:, ph * C : ph * C + C], x[...], (((0,), (0,)), ((), ())),
                preferred_element_type=F32,
            )

    picks = (((0, 0), (1, 0)), ((0, 1), (1, 0)), ((0, 1), (1, 1)))
    scale = 1.0 / 512.0
    for ka in range(3):
        for kb in range(3):
            for h in range(2):
                total = None
                for i, dr in picks[ka]:
                    for j, dq in picks[kb]:
                        lo = (2 * dr + dq) * C + h * 128
                        term = gt[2 * i + j, :, lo : lo + 128]
                        total = term if total is None else total + term
                total = total * scale
                dw[h, 3 * ka + kb] = total
                sa[h, 3 * ka + kb] = total.astype(BF16)
    move_a = remote(sa.at[1 - core], ra, a_ss.at[0], a_rs.at[0], (a, mate))
    move_a.start()

    z[16 : 16 + ROWS, :] = lax.dot_general(
        a_all[0:ROWS, :], wc[...], (((1,), (1,)), ((), ())), preferred_element_type=F32
    )
    move_a.wait()
    for tap in range(9):
        pair = (dw[core, tap] + ra[tap].astype(F32)).astype(BF16)
        if tap < 5:
            sb[:, tap] = pair.reshape(16, 16, 128)
        else:
            sx[tap - 5] = pair

    def copy_x(k):
        to = lax.rem(a + k, LAT)
        return remote(sx.at[to], rx.at[a], x_ss.at[to], x_rs.at[a], (to, b))

    def recv_x(k):
        fr = lax.rem(a + LAT - k, LAT)
        return remote(sx.at[fr], rx.at[fr], x_ss.at[fr], x_rs.at[fr], (fr, b))

    for k in range(1, LAT):
        copy_x(k).start()
    rx[a] = sx[a]

    def chip_copy(src, dst, ss, rs, k):
        to = lax.rem(chip + k, 16)
        return remote(src.at[to], dst.at[chip], ss.at[0], rs.at[0], (a, 2 * to + core))

    total = None
    for dr in range(2):
        for dq in range(2):
            at = 16 - dr * W - dq
            lo = (2 * dr + dq) * C
            term = z[at : at + ROWS, lo : lo + C]
            total = term if total is None else total + term
    cg[0:ROWS, :] = total.astype(BF16)
    sending = jnp.dot(gather_m[...], cg[...], preferred_element_type=F32)
    s3[...] = sending.astype(BF16).reshape(LON, 16, C)
    loop(1, LON, lambda k: lon_copy(s3, r3, s3_ss, s3_rs, k).start())
    r3[b] = s3[b]
    loop(1, 16, lambda k: chip_copy(sb, rb, b_ss, b_rs, k).start())
    rb[chip] = sb[chip]


    target_col = jnp.broadcast_to(target, (128, TOK)).astype(F32).T
    for blk in range(4):
        place_m[0:TOK, blk * 128 : blk * 128 + 128] = one_hot(
            target_col, (iota((TOK, 128), 1) + blk * 128).astype(F32)
        )

    def emit(t, carry):
        for i in range(2):
            at = (t + i) * (2 * W) + 1
            decoded[2 * t + i] = jnp.concatenate(
                [ct[i, 0, pl.ds(at, 16), :], ct[i, 1, pl.ds(at, 16), :]], axis=1
            ).astype(BF16)
        return carry

    lax.fori_loop(0, 64, emit, 0, unroll=4)

    for k in range(1, LAT):
        recv_x(k).wait_recv()
    whole = rx[0].astype(F32)
    for k in range(1, LAT):
        whole = whole + rx[k].astype(F32)
    sy[...] = whole.astype(BF16).reshape(16, 16, 128)
    loop(1, 16, lambda k: chip_copy(sy, ry, y_ss, y_rs, k).start())
    ry[chip] = sy[chip]

    group(s3, r3, s3_ss, s3_rs, LON - 1).wait_recv()
    back = jnp.dot(perm[1], r3[...].reshape(TOK, C), preferred_element_type=F32)
    s4[...] = back.astype(BF16).reshape(LAT, 128, C)

    def copy4(k):
        to = lax.rem(a + k, LAT)
        return remote(s4.at[to], r4.at[a], s4_ss.at[to], s4_rs.at[a], (to, b))

    def recv4(k):
        fr = lax.rem(a + LAT - k, LAT)
        return remote(s4.at[fr], r4.at[fr], s4_ss.at[fr], s4_rs.at[fr], (fr, b))

    for k in range(1, LAT):
        copy4(k).start()
    r4[a] = s4[a]

    group(sb, rb, b_ss, b_rs, 15).wait_recv()
    planes = []
    for tap in range(5):
        plane = rb[0, tap].astype(F32)
        for m in range(1, 16):
            plane = plane + rb[m, tap].astype(F32)
        planes.append(plane)
    group(sy, ry, y_ss, y_rs, 15).wait_recv()
    plane = ry[0].astype(F32)
    for m in range(1, 16):
        plane = plane + ry[m].astype(F32)
    planes.append(plane)
    for c in range(2):
        eight = slice(8 * c, 8 * c + 8)
        for n in range(3):
            sd[c, n] = jnp.concatenate(
                [planes[2 * n][eight, :], planes[2 * n + 1][eight, :]], axis=0
            ).astype(BF16)

    def pair_of(k, c):
        return lax.rem(a + k, LAT), lax.rem(core + c, 2)

    def copy_d(k, c):
        aa, cc = pair_of(k, c)
        return remote(
            sd.at[cc], rd.at[core, a], d_ss.at[cc, aa], d_rs.at[core, a], (aa, 2 * chip + cc)
        )

    def recv_d(k, c):
        aa, cc = pair_of(LAT - k, c)
        return remote(
            sd.at[cc], rd.at[cc, aa], d_ss.at[cc, aa], d_rs.at[cc, aa], (aa, 2 * chip + cc)
        )

    others = [(k, c) for c in range(2) for k in range(LAT) if (k, c) != (0, 0)]
    for k, c in others:
        copy_d(k, c).start()
    rd[core, a] = sd[core]

    for k in range(1, LAT):
        recv4(k).wait_recv()
    tgrad[...] = jnp.dot(
        place_m[0:TOK, :], r4[...].reshape(TOK, C), preferred_element_type=F32
    ).astype(BF16)

    for k, c in others:
        recv_d(k, c).wait_recv()
    for c in range(2):
        lanes = slice(c * 128, c * 128 + 128)
        for n in range(3):
            quad = [rd[c, k, n].astype(F32) for k in range(LAT)]
            total = (quad[0] + quad[1]) + (quad[2] + quad[3])
            wgrad[2 * n, :, lanes] = total[0:8, :]
            if n < 2:
                wgrad[2 * n + 1, :, lanes] = total[8:16, :]
        for k in range(LAT):
            wgrad[5 + k, :, lanes] = quad[k][8:16, :]

    for k in range(1, LAT):
        copy1(k).wait_send()
        copy4(k).wait_send()
    group(s2, r2, s2_ss, s2_rs, LON - 1).wait_send()
    group(s3, r3, s3_ss, s3_rs, LON - 1).wait_send()
    for k in range(1, LAT):
        copy_x(k).wait_send()
    group(sb, rb, b_ss, b_rs, 15).wait_send()
    group(sy, ry, y_ss, y_rs, 15).wait_send()
    for k, c in others:
        copy_d(k, c).wait_send()


def hand_over_kernel(decoded, wgrad, tgrad, decoded_out, wgrad_out, tgrad_out, sems):
    copies = [
        pltpu.make_async_copy(
            decoded.at[pl.ds(n * 32, 32)], decoded_out.at[pl.ds(n * 32, 32)], sems.at[n]
        )
        for n in range(4)
    ]
    copies.append(pltpu.make_async_copy(wgrad, wgrad_out, sems.at[4]))
    copies.append(pltpu.make_async_copy(tgrad, tgrad_out, sems.at[5]))
    for copy in copies:
        copy.start()
    for copy in copies:
        copy.wait()


def local(tokens, dest_tile, slot_cell, w_up, w_down, w_proj, w_conv, cotangent):
    vmem = pl.BlockSpec(memory_space=pltpu.VMEM)
    hbm = pl.BlockSpec(memory_space=pltpu.HBM)
    dma = pltpu.SemaphoreType.DMA
    v = pltpu.VMEM
    decoded, wgrad, tgrad = pl.pallas_call(
        grid_kernel,
        out_shape=(v((128, 16, C), BF16), v((9, 8, C), F32), v((TOK, C), BF16)),
        in_specs=[hbm] * 8,
        out_specs=(vmem, vmem, vmem),
        scratch_shapes=[
            v((TOK, D), BF16),
            v((RING, D, BLOCK), BF16),
            v((RING, BLOCK, D), BF16),
            v((TOK, D), BF16),
            v((TOK, D), F32),
            v((TOK, BLOCK), F32),
            v((TOK, BLOCK), F32),
            v((1, TOK), jnp.int32),
            v((CAP, 128), jnp.int32),
            v((D, C), BF16),
            v((9, C, C), BF16),
            v((128, 16, C), BF16),
            v((LAT, 128, C), BF16),
            dma((4,)), dma((RING,)), dma((RING,)), dma((5,)),
            v((LAT, 128, C), BF16),
            v((LON, 16, C), BF16),
            v((LON, 16, C), BF16),
            v((4 * C, 4 * C), BF16),
            v((3, 680, 128), F32),
            v((PADDED, 4 * C), BF16),
            v((2, 2, 2 * ROWS, 128), F32),
            v((PADDED, 4 * C), BF16),
            v((PADDED, 4 * C), BF16),
            v((16 + ROWS, 4 * C), F32),
            v((PADDED, C), BF16),
            v((4, C, 4 * C), F32),
            v((2, 9, C, 128), F32),
            v((2, 9, C, 128), BF16),
            v((9, C, 128), BF16),
            v((16, 5, 16, 128), BF16),
            v((16, 5, 16, 128), BF16),
            v((LAT, C, 128), BF16),
            v((LAT, C, 128), BF16),
            v((16, 16, 128), BF16),
            v((16, 16, 128), BF16),
            v((2, 3, 16, 128), BF16),
            v((2, LAT, 3, 16, 128), BF16),
            v((2, TOK, TOK), BF16),
            v((832, TOK), BF16),
            v((TOK, PADDED), BF16),
            v((160, C + 128), BF16),
            v((2, 64, C + 128), BF16),
            v((6, 16, C + 128), BF16),
            v((2, 128, C), BF16),
            v((2, 128, C), BF16),
            v((6, 16, C), BF16),
            v((LON, 16, C), BF16),
            v((LON, 16, C), BF16),
            v((LAT, 128, C), BF16),
            v((LAT, 128, C), BF16),
            dma((LAT,)), dma((LAT,)), dma((LON,)), dma((LON,)), dma((8,)), dma((8,)),
            dma((8,)), dma((8,)), dma((LON,)), dma((LON,)), dma((LAT,)), dma((LAT,)),
            dma((1,)), dma((1,)), dma((16,)), dma((16,)), dma((2, LAT)), dma((2, LAT)),
            dma((LAT,)), dma((LAT,)), dma((16,)), dma((16,)),
        ],
        compiler_params=pltpu.CompilerParams(
            collective_id=0, has_side_effects=True, vmem_limit_bytes=58 * 1024 * 1024
        ),
        cost_estimate=pl.CostEstimate(
            flops=22_000_000_000, bytes_accessed=24_000_000, transcendentals=2_600_000
        ),
        name="grid",
    )(
        tokens, dest_tile.reshape(1, TOK), slot_cell.reshape(LAT * LON, CAP).T, w_up, w_down, w_proj,
        w_conv.reshape(9, C, C), cotangent,
    )
    decoded, wgrad, tgrad = pl.pallas_call(
        hand_over_kernel,
        out_shape=(
            jax.ShapeDtypeStruct((128, 16, C), BF16),
            jax.ShapeDtypeStruct((9, 8, C), F32),
            jax.ShapeDtypeStruct((TOK, C), BF16),
        ),
        in_specs=[vmem] * 3,
        out_specs=(hbm, hbm, hbm),
        scratch_shapes=[dma((6,))],
        compiler_params=pltpu.CompilerParams(vmem_limit_bytes=1024 * 1024),
        name="hand_over",
    )(*(pltpu.with_memory_space_constraint(r, pltpu.VMEM) for r in (decoded, wgrad, tgrad)))
    weight_grad = wgrad.reshape(3, 3, 8, C).transpose(0, 1, 3, 2)
    return decoded, weight_grad, tgrad


def solution(mesh):
    in_specs = (
        P(("lat", "lon"), None),
        P(("lat", "lon")),
        P(("lat", "lon"), None, None),
        P(),
        P(),
        P(),
        P(),
        P("lat", "lon", None),
    )
    out_specs = (P("lat", "lon", None), P(None, None, None, "lon"), P(("lat", "lon"), None))
    return jax.shard_map(local, mesh=mesh, in_specs=in_specs, out_specs=out_specs, check_vma=False)
```
